32 devices in a mesh: width: 8 (over z, x), chan: 4 (over y, core).
Axes of the slice: x: 2, y: 2, z: 4, core: 2. Of those that a mesh axis runs over, the one named last changes fastest.
Arguments:
- activations: bfloat16 [512, 2, 6144], P('chan', None, 'width'), may hold values from -6 to 6
- filters: bfloat16 [512, 3, 3, 512], P('chan'), may hold values from -0.125 to 0.125
- cotangent: bfloat16 [512, 2, 6144], P('chan', None, 'width'), may hold values from -6 to 6
Outputs:
- conv_output: bfloat16 [512, 2, 6144], P('chan', None, 'width')
- input_grad: bfloat16 [512, 2, 6144], P('chan', None, 'width')
- filter_grad: float32 [512, 3, 3, 512], P('chan')
The draws below stay inside these ranges and needn't reach their ends.
All inputs are finite; a program needn't handle non-finite values.
Results may differ from the reference program's by a relative error of at most 0.001.
Values may be sent and summed in bfloat16 or wider, within the bound.
No kernel may reach another device: no remote copies, remote signals or barrier semaphores. Data moves between devices by JAX's collectives and lax.ppermute only.
A program may use at most 128 MiB of HBM per device.

```python
import math
import jax
import jax.numpy as jnp
from jax import lax

CIN = 512
COUT = 512
ROWS = 2
COLS = 6144


def spiked(entries, key, source, target, parts, factor):
    def block_of(dim):
        return (jnp.arange(entries.shape[dim]) // (entries.shape[dim] // parts)).reshape((-1,) + (1,) * (entries.ndim - 1 - dim))

    near = jax.random.permutation(key, parts)[block_of(target)]
    second = (block_of(target) + parts // 2) % parts
    return jnp.where((block_of(source) == near) | (block_of(source) == second), factor * entries, entries)


def block_levels(rng, shape, shards, least, top_value):
    loudness, own = 1.0, jax.random.fold_in(rng, 6)
    for dim, parts in shards:
        steps = jnp.exp(jax.random.uniform(jax.random.fold_in(own, dim), (parts,), jnp.float32, least / len(shards), top_value / len(shards)))
        loudness = loudness * jnp.repeat(steps, shape[dim] // parts).reshape([-1 if axis == dim else 1 for axis in range(len(shape))])
    return loudness


def gaussian(stream_key, extent, width, reach, shards=(), dtype=jnp.bfloat16):
    loudness = block_levels(stream_key, extent, shards, -0.22, 0.18) if shards else 1.0
    entries = jax.random.normal(stream_key, extent, jnp.float32) * width * loudness
    return jnp.minimum(jnp.maximum(entries, -reach), reach).astype(dtype)


def bell_draw_with(stream_key, extent, spread, bound, shards, heavy, kind=jnp.bfloat16):
    array = spread * jax.random.normal(stream_key, extent, jnp.float32)
    if shards:
        array = array * block_levels(stream_key, extent, shards, -0.22, 0.18)
    return jnp.clip(spiked(array, jax.random.fold_in(stream_key, 3), *heavy), -bound, bound).astype(kind)


def setup_inputs(seed: int = 0) -> dict:
    keys = jax.random.split(jax.random.key(seed), 4)
    activations = gaussian(keys[0], (CIN, ROWS, COLS), 1.0, 6.0, ((0, 4), (2, 8)))
    filters = bell_draw_with(keys[1], (CIN, 3, 3, COUT), (9 * CIN) ** -0.5, 0.125, ((0, 4),), (0, 3, 4, 2.0))
    cotangent = gaussian(keys[2], (COUT, ROWS, COLS), 1.0, 6.0, ((0, 4), (2, 8)))
    return {"activations": activations, "filters": filters, "cotangent": cotangent}


def tap_view(padded, tap_row, tap_col, rows, cols):
    return padded[:, tap_row:tap_row + rows, tap_col:tap_col + cols].reshape(padded.shape[0], rows * cols)

def reference(activations, filters, cotangent):
    rows = ROWS
    cols = COLS
    padded = jnp.pad(activations, ((0, 0), (1, 1), (1, 1)))
    grad_pad = jnp.pad(cotangent, ((0, 0), (1, 1), (1, 1)))
    flat_cot = cotangent.reshape(COUT, rows * cols)
    forward = jnp.zeros((COUT, rows * cols), jnp.float32)
    backward = jnp.zeros((CIN, rows * cols), jnp.float32)
    tap_grads = []
    for tap_row in range(3):
        for tap_col in range(3):
            kernel = filters[:, tap_row, tap_col, :]
            source = tap_view(padded, tap_row, tap_col, rows, cols)
            forward = forward + lax.dot_general(kernel, source, (((0,), (0,)), ((), ())), preferred_element_type=jnp.float32)
            backward = backward + jnp.dot(kernel, tap_view(grad_pad, 2 - tap_row, 2 - tap_col, rows, cols), preferred_element_type=jnp.float32)
            tap_grads.append(lax.dot_general(source, flat_cot, (((1,), (1,)), ((), ())), preferred_element_type=jnp.float32))
    factor = 1.0 / math.sqrt(rows * cols)
    filter_grad = jnp.stack(tap_grads, 1).reshape(CIN, 3, 3, COUT) * factor
    conv_output = forward.reshape(COUT, rows, cols).astype(jnp.bfloat16)
    input_grad = backward.reshape(CIN, rows, cols).astype(jnp.bfloat16)
    return (conv_output, input_grad, filter_grad)
```

```python
import functools
import math

import jax
import jax.numpy as jnp
from jax import lax
from jax.experimental import pallas as pl
from jax.experimental.pallas import tpu as pltpu
from jax.sharding import PartitionSpec as P

BF16, F16, F32 = jnp.bfloat16, jnp.float16, jnp.float32
TOP = 14.0
TAIL = 16
VMEM = pl.BlockSpec(memory_space=pltpu.VMEM)
NT = (((1,), (1,)), ((), ()))
TN = (((0,), (0,)), ((), ()))


def exchange(value, axis, bit):
    devices = lax.axis_size(axis)
    return lax.ppermute(value, axis, [(i, i ^ bit) for i in range(devices)])


def bits_of(devices):
    return devices.bit_length() - 1


def reversed_bits(index, count):
    out = 0
    for b in range(count):
        out = out + (((index >> b) & 1) << (count - 1 - b))
    return out


def call(body, name, outs, scratch, flops, *args):
    outs = [jax.ShapeDtypeStruct(shape, dtype) for shape, dtype in outs]
    moved = sum(a.size * a.dtype.itemsize for a in list(args) + outs)
    result = pl.pallas_call(
        body,
        out_shape=outs,
        in_specs=[VMEM] * len(args),
        out_specs=[VMEM] * len(outs),
        scratch_shapes=[pltpu.VMEM(shape, dtype) for shape, dtype in scratch],
        compiler_params=pltpu.CompilerParams(vmem_limit_bytes=32 << 20),
        cost_estimate=pl.CostEstimate(flops=flops, bytes_accessed=moved, transcendentals=0),
        name=name,
    )(*args)
    return result[0] if len(outs) == 1 else result


def taps_kernel(x, before, after, out):
    chans, rows, cols = x.shape
    edge = before.shape[2]
    for i in range(rows):
        row = jnp.concatenate([before[:, i, :], x[:, i, :], after[:, i, :]], axis=1)
        for b in range(3):
            first = edge - 1 + b
            out[i, b * chans : (b + 1) * chans, :] = row[:, first : first + cols]


def filter_kernel(factor, piece, xs, ga, gb, send, keep, gsc, acc):
    rows, deep, cols = xs.shape
    width = lax.axis_size("width")
    nbits = bits_of(width)
    block = ga.shape[1]
    parity = lax.axis_index("chan") & 1
    gsc[:, pl.ds(pl.multiple_of(parity * block, block), block), :] = ga[...]
    gsc[:, pl.ds(pl.multiple_of((1 - parity) * block, block), block), :] = gb[...]
    for a in range(3):
        total = None
        for h in range(rows):
            i = h + a - 1
            if 0 <= i < rows:
                part = lax.dot_general(xs[i], gsc[h], NT, preferred_element_type=F32)
                total = part if total is None else total + part
        acc[a * deep : (a + 1) * deep, :] = total * factor
    if acc.shape[0] > 3 * deep:
        acc[3 * deep :, :] = jnp.zeros((acc.shape[0] - 3 * deep, acc.shape[1]), F32)
    most = jnp.max(jnp.abs(acc[...]), axis=(0, 1), keepdims=True)
    power = jnp.ceil(jnp.log2(jnp.maximum(most, 2.0**-110)))
    mine = reversed_bits(lax.axis_index("width"), nbits)
    half = width // 2
    for r in range(width):
        rows_of = acc[pl.ds(pl.multiple_of((mine ^ r) * piece, 16), piece), :]
        if r < half:
            keep[r * piece : (r + 1) * piece, :] = rows_of
        else:
            send[(r - half) * piece : (r - half + 1) * piece, :] = rows_of * jnp.exp2(TOP - power)
    send[half * piece :, :] = jnp.broadcast_to(power, (TAIL, acc.shape[1]))
    keep[half * piece :, :] = jnp.broadcast_to(power, (TAIL, acc.shape[1]))


def forward_kernel(xs, f, send, keep, acc):
    rows, deep, cols = xs.shape
    groups = lax.axis_size("chan")
    nbits = bits_of(groups)
    block = acc.shape[0] // groups
    me = lax.axis_index("chan")
    for h in range(rows):
        total = None
        for i in range(max(0, h - 1), min(rows, h + 2)):
            part = lax.dot_general(f[i - h + 1], xs[i], TN, preferred_element_type=F32)
            total = part if total is None else total + part
        acc[...] = total
        for q in range(groups):
            owner = me ^ reversed_bits(q, nbits)
            rows_of = acc[pl.ds(pl.multiple_of(owner * block, block), block), :]
            if q < groups // 2:
                keep[q, h] = rows_of
            else:
                send[q - groups // 2, h] = rows_of


def input_kernel(f, edge_rows, *refs):
    groups = lax.axis_size("chan")
    gs, (out, gsc, hsc) = refs[:groups], refs[groups:]
    rows, block, cols = gs[0].shape
    chans = out.shape[1]
    me = lax.axis_index("chan")
    for r in range(groups):
        at = pl.ds(pl.multiple_of((me ^ r) * block, block), block)
        gsc[:, at, :] = gs[r][...]
        if block % 128 == 0:
            hsc[:, at] = edge_rows[r]
    if block % 128:
        hsc[...] = edge_rows[...]
    lane = lax.broadcasted_iota(jnp.int32, (chans, cols), 1)
    sums = [None] * rows
    for i in range(rows):
        taps = [a for a in range(3) if 0 <= a - 1 + i < rows]
        mats = f[taps[0] * 3 * chans : (taps[-1] + 1) * 3 * chans, :]
        prod = jnp.dot(mats, gsc[i], preferred_element_type=F32)
        ends = lax.dot_general(mats, hsc[...], NT, preferred_element_type=F32)
        for n, a in enumerate(taps):
            h = a - 1 + i
            for b in range(3):
                at = slice((n * 3 + b) * chans, (n * 3 + b + 1) * chans)
                term = prod[at]
                if b == 0:
                    term = jnp.where(lane == cols - 1, ends[at, 2 * i + 1 : 2 * i + 2], pltpu.roll(term, cols - 1, 1))
                elif b == 2:
                    term = jnp.where(lane == 0, ends[at, 2 * i : 2 * i + 1], pltpu.roll(term, 1, 1))
                sums[h] = term if sums[h] is None else sums[h] + term
    for h in range(rows):
        out[h] = sums[h].astype(BF16)


def packed(values, power):
    tail = jnp.broadcast_to(power, (TAIL, values.shape[1]))
    return jnp.concatenate([values * jnp.exp2(TOP - power), tail], axis=0).astype(F16)


def reduce_pieces(send, keep):
    power = keep[-1:, :1]
    total = keep[:-TAIL]
    message = send.astype(F16)
    for b in range(bits_of(lax.axis_size("width"))):
        got = exchange(message, "width", 1 << b)
        count = got.shape[0] - TAIL
        other = got[count : count + 1, :1].astype(F32)
        total = total[:count] + got[:count].astype(F32) * jnp.exp2(other - TOP)
        power = jnp.maximum(power, other) + 1.0
        left = count // 2 if 2 << b < lax.axis_size("width") else 0
        message = packed(total[left:], power)
    return message


def gather_pieces(message):
    me = lax.axis_index("width")
    every = message[None]
    for b in reversed(range(bits_of(lax.axis_size("width")))):
        got = exchange(every, "width", 1 << b)
        late = ((me >> b) & 1) == 1
        every = jnp.concatenate([jnp.where(late, got, every), jnp.where(late, every, got)], axis=0)
    return every


def unpacked(every):
    rows = every.shape[1] - TAIL
    scale = jnp.exp2(every[:, rows : rows + 1].astype(F32) - TOP)
    return (every[:, :rows].astype(F32) * scale).reshape(-1, every.shape[2])


def body(activations, filters, cotangent):
    chans, rows, cols = activations.shape
    block = cotangent.shape[0]
    outs = filters.shape[3]
    groups, width = lax.axis_size("chan"), lax.axis_size("width")
    me = lax.axis_index("chan")
    up = [(i, i + 1) for i in range(width - 1)]
    down = [(i + 1, i) for i in range(width - 1)]
    edge = min(128, cols)

    g = {0: jnp.transpose(cotangent, (1, 0, 2))}
    for b in reversed(range(bits_of(groups))):
        for r in sorted(g):
            g[r | 1 << b] = exchange(g[r], "chan", 1 << b)

    before = lax.ppermute(activations[:, :, cols - edge :], "width", up)
    after = lax.ppermute(activations[:, :, :edge], "width", down)
    xs = call(taps_kernel, "shifted_taps", [((rows, 3 * chans, cols), BF16)], [], 0, activations, before, after)

    mats = jnp.transpose(filters, (1, 2, 0, 3))
    pairs_of_rows = sum(0 <= h + a - 1 < rows for h in range(rows) for a in range(3))
    flops = 2 * pairs_of_rows * 3 * chans * cols * outs

    piece = -(-9 * chans // width)
    piece = -(-piece // 16) * 16
    factor = 1.0 / math.sqrt(rows * cols * width)
    share = (width // 2 * piece + TAIL, 2 * block)
    pieces = []
    for j in range(groups // 2):
        send, keep = call(
            functools.partial(filter_kernel, factor, piece),
            "filter_terms",
            [(share, F32), (share, F32)],
            [((rows, 2 * block, cols), BF16), ((width * piece, 2 * block), F32)],
            flops * 2 // groups,
            xs,
            g[2 * j],
            g[2 * j + 1],
        )
        pieces.append(gather_pieces(reduce_pieces(send, keep)))

    send, keep = call(
        forward_kernel,
        "forward_terms",
        [((groups // 2, rows, block, cols), F32)] * 2,
        [((outs, cols), F32)],
        flops,
        xs,
        mats.reshape(3, 3 * chans, outs),
    )
    for b in range(bits_of(groups)):
        total = keep + exchange(send, "chan", 1 << b)
        keep, send = total[: total.shape[0] // 2], total[total.shape[0] // 2 :]
    conv_output = jnp.transpose(total[0].astype(BF16), (1, 0, 2))

    firsts = jnp.stack([g[r][:, :, 0] for r in range(groups)])
    lasts = jnp.stack([g[r][:, :, -1] for r in range(groups)])
    left = lax.ppermute(lasts, "width", up)
    right = lax.ppermute(firsts, "width", down)
    ends = jnp.stack([left, right], axis=2).reshape(groups, 2 * rows, block)
    ends = jnp.pad(ends, ((0, 0), (0, 16 - 2 * rows), (0, 0)))
    if block % 128:
        order = me ^ jnp.arange(groups)
        ends = jnp.transpose(ends[order], (1, 0, 2)).reshape(16, outs)
    input_grad = call(
        input_kernel,
        "input_terms",
        [((rows, chans, cols), BF16)],
        [((rows, outs, cols), BF16), ((16, outs), BF16)],
        flops,
        mats.reshape(9 * chans, outs),
        ends,
        *[g[r] for r in range(groups)],
    )
    input_grad = jnp.transpose(input_grad, (1, 0, 2))

    for b in range(bits_of(groups // 2)):
        swap = ((me >> (b + 1)) & 1) == 1
        pieces = [jnp.where(swap, pieces[j ^ 1 << b], pieces[j]) for j in range(len(pieces))]
    grads = jnp.concatenate([unpacked(p) for p in pieces], axis=1)[: 9 * chans]
    grads = jnp.transpose(grads.reshape(3, 3, chans, outs), (2, 0, 1, 3))
    return conv_output, input_grad, grads


def solution(mesh):
    cols = P("chan", None, "width")
    mats = P("chan", None, None, None)
    return jax.shard_map(body, mesh=mesh, in_specs=(cols, mats, cols), out_specs=(cols, cols, mats), check_vma=False)
```

```python
import functools
import math

import jax
import jax.numpy as jnp
from jax import lax
from jax.experimental import pallas as pl
from jax.experimental.pallas import tpu as pltpu
from jax.sharding import PartitionSpec as P

BF16, F16, F32 = jnp.bfloat16, jnp.float16, jnp.float32
LANES = 128
TOP = 14.0
LEAST = 2.0**-110
POWER = 8
EDGE = 8
VMEM = pl.BlockSpec(memory_space=pltpu.VMEM)
NT = (((1,), (1,)), ((), ()))
TN = (((0,), (0,)), ((), ()))


def exchange(value, axis, bit):
    devices = lax.axis_size(axis)
    return lax.ppermute(value, axis, [(i, i ^ bit) for i in range(devices)])


def bits_of(devices):
    return devices.bit_length() - 1


def reversed_bits(index, count):
    out = 0
    for b in range(count):
        out = out + (((index >> b) & 1) << (count - 1 - b))
    return out


def call(body, name, outs, scratch, flops, *args):
    outs = [jax.ShapeDtypeStruct(shape, dtype) for shape, dtype in outs]
    moved = sum(a.size * a.dtype.itemsize for a in list(args) + outs)
    result = pl.pallas_call(
        body,
        out_shape=outs,
        in_specs=[VMEM] * len(args),
        out_specs=[VMEM] * len(outs),
        scratch_shapes=[pltpu.VMEM(shape, dtype) for shape, dtype in scratch],
        compiler_params=pltpu.CompilerParams(vmem_limit_bytes=16 << 20),
        cost_estimate=pl.CostEstimate(flops=flops, bytes_accessed=moved, transcendentals=0),
        name=name,
    )(*args)
    return result[0] if len(outs) == 1 else result


def exponent(values):
    most = jnp.max(jnp.abs(values), axis=(0, 1), keepdims=True)
    return jnp.ceil(jnp.log2(jnp.maximum(most, LEAST)))


def taps_kernel(x, *refs):
    *ends, out = refs
    chans, rows, cols = x.shape
    if ends:
        tiles = ends[0].shape[0]
        tile = lax.axis_index("width")
        left = ends[0][jnp.maximum(tile - 1, 0)]
        right = ends[0][jnp.minimum(tile + 1, tiles - 1)]
        left = jnp.where(tile > 0, left[3:4] * jnp.exp2(left[0:1] - TOP), 0.0)
        right = jnp.where(tile < tiles - 1, right[2:3] * jnp.exp2(right[0:1] - TOP), 0.0)
        row_of = lax.broadcasted_iota(jnp.int32, (16, LANES), 0)
        lane = lax.broadcasted_iota(jnp.int32, (16, LANES), 1)
        place = ((row_of == 0) & (lane == LANES - 1)) | ((row_of == 1) & (lane == 0))
        place = jnp.where(place, 1.0, 0.0).astype(BF16)
    for i in range(rows):
        side = jnp.zeros((chans, LANES), BF16)
        if ends:
            at = slice(i * chans, (i + 1) * chans)
            both = jnp.concatenate([left[:, at], right[:, at], jnp.zeros((14, chans), F32)], axis=0).astype(BF16)
            side = lax.dot_general(both, place, TN, preferred_element_type=F32).astype(BF16)
        row = jnp.concatenate([side, x[:, i, :], side], axis=1)
        for b in range(3):
            out[i, b * chans : (b + 1) * chans, :] = row[:, LANES - 1 + b : LANES - 1 + b + cols]


def filter_kernel(factor, piece, first, xs, ga, gb, send, keep, gsc, acc):
    rows, deep, cols = xs.shape
    chans = deep // 3
    width = lax.axis_size("width")
    block = ga.shape[1]
    lanes = 2 * block
    parity = lax.axis_index("chan") & 1
    gsc[:, pl.ds(pl.multiple_of(parity * block, block), block), :] = ga[...]
    gsc[:, pl.ds(pl.multiple_of((1 - parity) * block, block), block), :] = gb[...]
    for a in range(3):
        total = None
        for h in range(rows):
            i = h + a - 1
            if 0 <= i < rows:
                part = lax.dot_general(xs[i], gsc[h], NT, preferred_element_type=F32)
                total = part if total is None else total + part
        acc[a * deep : (a + 1) * deep, :] = total * factor
    if acc.shape[0] > 3 * deep:
        acc[3 * deep :, :] = jnp.zeros((acc.shape[0] - 3 * deep, lanes), F32)
    power = exponent(acc[...])
    mine = reversed_bits(lax.axis_index("width"), bits_of(width))
    half = width // 2
    for r in range(width):
        rows_of = acc[pl.ds(pl.multiple_of((mine ^ r) * piece, 16), piece), :]
        if r < half:
            keep[r * piece : (r + 1) * piece, :] = rows_of
        else:
            send[(r - half) * piece : (r - half + 1) * piece, :] = rows_of * jnp.exp2(TOP - power)
    power = jnp.broadcast_to(power, (POWER, lanes))
    send[half * piece : half * piece + POWER, :] = power
    keep[half * piece :, :] = power
    row_of = lax.broadcasted_iota(jnp.int32, (16, cols), 0)
    lane = lax.broadcasted_iota(jnp.int32, (16, cols), 1)
    pick = ((row_of == 0) & (lane == 0)) | ((row_of == 1) & (lane == cols - 1))
    pick = jnp.where(pick, 1.0, 0.0).astype(BF16)
    gends = [lax.dot_general(pick, gsc[h], NT, preferred_element_type=F32) for h in range(rows)]
    gends = jnp.concatenate([gends[h][s : s + 1] for s in range(2) for h in range(rows)], axis=0)
    if first:
        xends = [lax.dot_general(pick, xs[i, chans : 2 * chans], NT, preferred_element_type=F32) for i in range(rows)]
        xends = jnp.concatenate([v[:2] for v in xends], axis=1)
    else:
        xends = jnp.zeros((2, lanes), F32)
    xpower, gpower = exponent(xends), exponent(gends)
    send[half * piece + POWER :, :] = jnp.concatenate(
        [
            jnp.broadcast_to(xpower, (1, lanes)),
            jnp.broadcast_to(gpower, (1, lanes)),
            xends * jnp.exp2(TOP - xpower),
            gends * jnp.exp2(TOP - gpower),
        ],
        axis=0,
    )


def border_kernel(factor, total, xends, gends, out, acc):
    tiles, _, lanes = gends.shape
    piece = total.shape[0]
    rows = 2
    chans = lanes // rows
    tile = lax.broadcasted_iota(jnp.int32, (tiles, lanes), 0)

    def decoded(ref, kind, power):
        return ref[:, kind, :] * jnp.exp2(ref[:, power, :] - TOP)

    before = jnp.where(tile == 0, 0.0, pltpu.roll(decoded(xends, 3, 0), 1, 0))
    behind = jnp.where(tile == tiles - 1, 0.0, pltpu.roll(decoded(xends, 2, 0), tiles - 1, 0))
    acc[...] = jnp.zeros(acc.shape, F32)
    for b, source, kind in ((0, before, 4), (2, behind, 4 + rows)):
        grads = jnp.concatenate([decoded(gends, kind + h, 1) for h in range(rows)], axis=0).astype(BF16)
        nothing = jnp.zeros((tiles, chans), F32)
        for a in range(3):
            taken = [h + a - 1 for h in range(rows)]
            taken = [source[:, i * chans : (i + 1) * chans] if 0 <= i < rows else nothing for i in taken]
            terms = lax.dot_general(jnp.concatenate(taken, axis=0).astype(BF16), grads, TN, preferred_element_type=F32)
            acc[(3 * a + b) * chans : (3 * a + b + 1) * chans, :] = terms * factor
    mine = reversed_bits(lax.axis_index("width"), bits_of(tiles))
    value = total[...] + acc[pl.ds(pl.multiple_of(mine * piece, 16), piece), :]
    power = exponent(value)
    out[:piece, :] = value * jnp.exp2(TOP - power)
    out[piece:, :] = jnp.broadcast_to(power, (POWER, lanes))


def forward_kernel(xs, f, send, keep, acc):
    rows, deep, cols = xs.shape
    groups = lax.axis_size("chan")
    nbits = bits_of(groups)
    block = acc.shape[0] // groups
    me = lax.axis_index("chan")
    for h in range(rows):
        total = None
        for i in range(max(0, h - 1), min(rows, h + 2)):
            part = lax.dot_general(f[i - h + 1], xs[i], TN, preferred_element_type=F32)
            total = part if total is None else total + part
        acc[...] = total
        for q in range(groups):
            owner = me ^ reversed_bits(q, nbits)
            rows_of = acc[pl.ds(pl.multiple_of(owner * block, block), block), :]
            if q < groups // 2:
                keep[q, h] = rows_of
            else:
                send[q - groups // 2, h] = rows_of


def input_kernel(f, ends, *refs):
    groups = lax.axis_size("chan")
    gs, (out, gsc, hsc) = refs[:groups], refs[groups:]
    rows, block, cols = gs[0].shape
    chans = out.shape[1]
    tiles = ends.shape[1]
    lanes = 2 * block
    me, tile = lax.axis_index("chan"), lax.axis_index("width")
    for r in range(groups):
        gsc[:, pl.ds(pl.multiple_of((me ^ r) * block, block), block), :] = gs[r][...]
    for q in range(groups // 2):
        left = ends[(me >> 1) ^ q, jnp.maximum(tile - 1, 0)]
        right = ends[(me >> 1) ^ q, jnp.minimum(tile + 1, tiles - 1)]
        left = jnp.where(tile > 0, left * jnp.exp2(left[1:2] - TOP), 0.0)
        right = jnp.where(tile < tiles - 1, right * jnp.exp2(right[1:2] - TOP), 0.0)
        both = jnp.concatenate([left[4 + rows :], right[4 : 4 + rows], jnp.zeros((16 - 2 * rows, lanes), F32)], axis=0)
        hsc[:, q * lanes : (q + 1) * lanes] = both.astype(BF16)
    lane = lax.broadcasted_iota(jnp.int32, (chans, cols), 1)
    sums = [None] * rows
    for i in range(rows):
        taps = [a for a in range(3) if 0 <= a - 1 + i < rows]
        mats = f[taps[0] * 3 * chans : (taps[-1] + 1) * 3 * chans, :]
        prod = jnp.dot(mats, gsc[i], preferred_element_type=F32)
        sides = lax.dot_general(mats, hsc[...], NT, preferred_element_type=F32)
        for n, a in enumerate(taps):
            h = a - 1 + i
            for b in range(3):
                at = slice((n * 3 + b) * chans, (n * 3 + b + 1) * chans)
                term = prod[at]
                if b == 0:
                    term = jnp.where(lane == cols - 1, sides[at, rows + i : rows + i + 1], pltpu.roll(term, cols - 1, 1))
                elif b == 2:
                    term = jnp.where(lane == 0, sides[at, i : i + 1], pltpu.roll(term, 1, 1))
                sums[h] = term if sums[h] is None else sums[h] + term
    for h in range(rows):
        out[h] = sums[h].astype(BF16)


class Order:
    def __init__(self):
        self.last = None

    def __call__(self, value):
        if self.last is not None:
            value, _ = lax.optimization_barrier((value, self.last))
        self.last = value
        return value


def doubled(got, own, bit):
    late = (lax.axis_index("width") & bit) != 0
    return jnp.concatenate([jnp.where(late, got, own), jnp.where(late, own, got)], axis=0)


def chunk_stages(send, keep, finish, order):
    steps = bits_of(lax.axis_size("width"))
    lanes = send.shape[1]
    total, power = keep[:-POWER], keep[-1:]
    message = send.astype(F16)
    ends = message[-EDGE:][None]
    for b in range(steps):
        got = exchange(order(message), "width", 1 << b)
        yield None
        got = order(got)
        count = total.shape[0]
        other = got[count : count + 1].astype(F32)
        total = total + got[:count].astype(F32) * jnp.exp2(other - TOP)
        power = jnp.maximum(power, other) + 1.0
        ends = doubled(got[count + POWER :].reshape(-1, EDGE, lanes), ends, 1 << b)
        if b < steps - 1:
            scaled = total[count // 2 :] * jnp.exp2(TOP - power)
            tail = jnp.broadcast_to(power, (POWER, lanes))
            message = jnp.concatenate([scaled.astype(F16), tail.astype(F16), ends.reshape(-1, lanes)], axis=0)
            total = total[: count // 2]
    every = finish(total, ends.astype(F32)).astype(F16)[None]
    for b in reversed(range(steps)):
        got = exchange(order(every), "width", 1 << b)
        yield None
        every = doubled(order(got), every, 1 << b)
    yield every


def unpacked(every):
    rows = every.shape[1] - POWER
    scale = jnp.exp2(every[:, rows : rows + 1].astype(F32) - TOP)
    return (every[:, :rows].astype(F32) * scale).reshape(-1, every.shape[2])


def chunk_times(chunks, steps):
    times = []
    for j in range(chunks):
        now = 2.6 * j
        for step in range(2 * steps + 1):
            times.append((now, j))
            now += 2.0 if step in (0, 2 * steps - 1) else 1.0
    return sorted(times)


def body(activations, filters, cotangent):
    chans, rows, cols = activations.shape
    block = cotangent.shape[0]
    outs = filters.shape[3]
    groups, width = lax.axis_size("chan"), lax.axis_size("width")
    me = lax.axis_index("chan")
    lanes = 2 * block
    mats = jnp.transpose(filters, (1, 2, 0, 3))
    pairs_of_rows = sum(0 <= h + a - 1 < rows for h in range(rows) for a in range(3))
    flops = 2 * pairs_of_rows * 3 * chans * cols * outs
    piece = -(-9 * chans // width)
    piece = -(-piece // 16) * 16
    factor = 1.0 / math.sqrt(rows * cols * width)
    order = Order()
    ends = {}

    def shifted(*sides):
        return call(taps_kernel, "shifted_taps", [((rows, 3 * chans, cols), BF16)], [], 0, activations, *sides)

    def filter_chunk(j):
        send, keep = call(
            functools.partial(filter_kernel, factor, piece, j == 0),
            "filter_terms",
            [((width // 2 * piece + POWER + EDGE, lanes), F32), ((width // 2 * piece + POWER, lanes), F32)],
            [((rows, lanes, cols), BF16), ((width * piece, lanes), F32)],
            flops * 2 // groups,
            bare,
            g[2 * j],
            g[2 * j + 1],
        )

        def finish(total, arrived):
            ends[j] = arrived
            body = functools.partial(border_kernel, factor)
            shape = ((piece + POWER, lanes), F32)
            return call(body, "border_terms", [shape], [((width * piece, lanes), F32)], 0, total, ends[0], ends[j])

        return chunk_stages(send, keep, finish, order)

    def forward():
        send, keep = call(
            forward_kernel,
            "forward_terms",
            [((groups // 2, rows, block, cols), F32)] * 2,
            [((outs, cols), F32)],
            flops,
            shifted(order(ends[0])),
            mats.reshape(3, 3 * chans, outs),
        )
        for b in range(bits_of(groups)):
            got = exchange(order(send), "chan", 1 << b)
            yield None
            total = keep + order(got)
            keep, send = total[: total.shape[0] // 2], total[total.shape[0] // 2 :]
        yield jnp.transpose(total[0].astype(BF16), (1, 0, 2))

    def backward():
        out = call(
            input_kernel,
            "input_terms",
            [((rows, chans, cols), BF16)],
            [((rows, outs, cols), BF16), ((16, outs), BF16)],
            flops,
            mats.reshape(9 * chans, outs),
            jnp.stack([order(ends[j]) for j in range(groups // 2)]),
            *[g[r] for r in range(groups)],
        )
        return jnp.transpose(out, (1, 0, 2))

    g = {0: order(jnp.transpose(cotangent, (1, 0, 2)))}
    g[1] = exchange(g[0], "chan", 1)
    for b in reversed(range(1, bits_of(groups))):
        for r in [r for r in sorted(g) if r != 1]:
            g[r | 1 << b] = exchange(g[r], "chan", 1 << b)
    bare = shifted()
    chunks = [filter_chunk(0)]
    next(chunks[0])
    for r in sorted(g):
        if r > 1:
            g[r | 1] = exchange(order(g[r]), "chan", 1)
    pieces = [None] * (groups // 2)
    conv = forward()
    waits = bits_of(groups) + 1
    for now, j in chunk_times(groups // 2, bits_of(width))[1:]:
        if j == len(chunks):
            g[2 * j + 1] = order(g[2 * j + 1])
            chunks.append(filter_chunk(j))
        pieces[j] = next(chunks[j])
        if 0 in ends and waits > 1 and (waits > bits_of(groups) or now > 6.2):
            conv_output = next(conv)
            waits -= 1
    input_grad = backward()
    while waits:
        conv_output = next(conv)
        waits -= 1

    for b in range(bits_of(groups // 2)):
        swap = ((me >> (b + 1)) & 1) == 1
        pieces = [jnp.where(swap, pieces[j ^ 1 << b], pieces[j]) for j in range(len(pieces))]
    grads = jnp.concatenate([unpacked(p) for p in pieces], axis=1)[: 9 * chans]
    grads = jnp.transpose(grads.reshape(3, 3, chans, outs), (2, 0, 1, 3))
    return conv_output, input_grad, grads


def solution(mesh):
    cols = P("chan", None, "width")
    mats = P("chan", None, None, None)
    return jax.shard_map(body, mesh=mesh, in_specs=(cols, mats, cols), out_specs=(cols, cols, mats), check_vma=False)
```

```python
import functools
import math

import jax
import jax.numpy as jnp
from jax import lax
from jax.experimental import pallas as pl
from jax.experimental.pallas import tpu as pltpu
from jax.sharding import PartitionSpec as P

BF16, F16, F32 = jnp.bfloat16, jnp.float16, jnp.float32
LANES = 128
TOP = 14.0
LEAST = 2.0**-110
POWER = 8
EDGE = 8
VMEM = pl.BlockSpec(memory_space=pltpu.VMEM)
NT = (((1,), (1,)), ((), ()))
TN = (((0,), (0,)), ((), ()))


def exchange(value, axis, bit):
    devices = lax.axis_size(axis)
    return lax.ppermute(value, axis, [(i, i ^ bit) for i in range(devices)])


def bits_of(devices):
    return devices.bit_length() - 1


def reversed_bits(index, count):
    out = 0
    for b in range(count):
        out = out + (((index >> b) & 1) << (count - 1 - b))
    return out


def piece_of(tile, tiles):
    return (tile & 1) * (tiles // 2) + (tile >> 1)


def call(body, name, outs, scratch, flops, *args):
    outs = [jax.ShapeDtypeStruct(shape, dtype) for shape, dtype in outs]
    moved = sum(a.size * a.dtype.itemsize for a in list(args) + outs)
    result = pl.pallas_call(
        body,
        out_shape=outs,
        in_specs=[VMEM] * len(args),
        out_specs=[VMEM] * len(outs),
        scratch_shapes=[pltpu.VMEM(shape, dtype) for shape, dtype in scratch],
        compiler_params=pltpu.CompilerParams(vmem_limit_bytes=16 << 20),
        cost_estimate=pl.CostEstimate(flops=flops, bytes_accessed=moved, transcendentals=0),
        name=name,
    )(*args)
    return result[0] if len(outs) == 1 else result


def exponent(values):
    most = jnp.max(jnp.abs(values), axis=(0, 1), keepdims=True)
    return jnp.ceil(jnp.log2(jnp.maximum(most, LEAST)))


def pick_columns(cols):
    row_of = lax.broadcasted_iota(jnp.int32, (16, cols), 0)
    lane = lax.broadcasted_iota(jnp.int32, (16, cols), 1)
    pick = ((row_of == 0) & (lane == 0)) | ((row_of == 1) & (lane == cols - 1))
    return jnp.where(pick, 1.0, 0.0).astype(BF16)


def taps_kernel(x, *refs):
    *sides, out, columns = refs
    chans, rows, cols = x.shape
    row_of = lax.broadcasted_iota(jnp.int32, (16, LANES), 0)
    lane = lax.broadcasted_iota(jnp.int32, (16, LANES), 1)
    place = ((row_of == 0) & (lane == LANES - 1)) | ((row_of == 1) & (lane == 0))
    place = jnp.where(place, 1.0, 0.0).astype(BF16)
    for i in range(rows):
        side = jnp.zeros((chans, LANES), BF16)
        if sides:
            both = [side_ref[...].astype(F32)[:, i * chans : (i + 1) * chans] for side_ref in sides]
            both = jnp.concatenate(both + [jnp.zeros((14, chans), F32)], axis=0).astype(BF16)
            side = lax.dot_general(both, place, TN, preferred_element_type=F32).astype(BF16)
        row = jnp.concatenate([side, x[:, i, :], side], axis=1)
        for b in range(3):
            out[i, b * chans : (b + 1) * chans, :] = row[:, LANES - 1 + b : LANES - 1 + b + cols]
        for at, tile in ((0, x[:, i, :LANES]), (1, x[:, i, cols - LANES :])):
            line = lax.dot_general(pick_columns(LANES), tile, NT, preferred_element_type=F32).astype(BF16)
            columns[at : at + 1, i * chans : (i + 1) * chans] = line[at : at + 1]


def filter_kernel(factor, piece, first, xs, ga, gb, send, keep, gsc, acc):
    rows, deep, cols = xs.shape
    chans = deep // 3
    width = lax.axis_size("width")
    block = ga.shape[1]
    lanes = 2 * block
    parity = lax.axis_index("chan") & 1
    gsc[:, pl.ds(pl.multiple_of(parity * block, block), block), :] = ga[...]
    gsc[:, pl.ds(pl.multiple_of((1 - parity) * block, block), block), :] = gb[...]
    for a in range(3):
        total = None
        for h in range(rows):
            i = h + a - 1
            if 0 <= i < rows:
                part = lax.dot_general(xs[i], gsc[h], NT, preferred_element_type=F32)
                total = part if total is None else total + part
        acc[a * deep : (a + 1) * deep, :] = total * factor
    if acc.shape[0] > 3 * deep:
        acc[3 * deep :, :] = jnp.zeros((acc.shape[0] - 3 * deep, lanes), F32)
    power = exponent(acc[...])
    mine = piece_of(lax.axis_index("width"), width)
    half = width // 2
    for r in range(width):
        rows_of = acc[pl.ds(pl.multiple_of((mine ^ r) * piece, 16), piece), :]
        if r < half:
            keep[r * piece : (r + 1) * piece, :] = rows_of
        else:
            send[(r - half) * piece : (r - half + 1) * piece, :] = rows_of * jnp.exp2(TOP - power)
    power = jnp.broadcast_to(power, (POWER, lanes))
    send[half * piece : half * piece + POWER, :] = power
    keep[half * piece :, :] = power
    pick = pick_columns(cols)
    gends = [lax.dot_general(pick, gsc[h], NT, preferred_element_type=F32) for h in range(rows)]
    gends = jnp.concatenate([gends[h][s : s + 1] for s in range(2) for h in range(rows)], axis=0)
    if first:
        xends = [lax.dot_general(pick, xs[i, chans : 2 * chans], NT, preferred_element_type=F32) for i in range(rows)]
        xends = jnp.concatenate([v[:2] for v in xends], axis=1)
    else:
        xends = jnp.zeros((2, lanes), F32)
    xpower, gpower = exponent(xends), exponent(gends)
    send[half * piece + POWER :, :] = jnp.concatenate(
        [
            jnp.broadcast_to(xpower, (1, lanes)),
            jnp.broadcast_to(gpower, (1, lanes)),
            xends * jnp.exp2(TOP - xpower),
            gends * jnp.exp2(TOP - gpower),
        ],
        axis=0,
    )


def border_kernel(factor, total, xends, gends, out, acc):
    tiles, _, lanes = gends.shape
    piece = total.shape[0]
    rows = 2
    chans = lanes // rows
    tile = lax.broadcasted_iota(jnp.int32, (tiles, lanes), 0)

    def decoded(ref, kind, power):
        return ref[:, kind, :] * jnp.exp2(ref[:, power, :] - TOP)

    before = jnp.where(tile == 0, 0.0, pltpu.roll(decoded(xends, 3, 0), 1, 0))
    behind = jnp.where(tile == tiles - 1, 0.0, pltpu.roll(decoded(xends, 2, 0), tiles - 1, 0))
    acc[...] = jnp.zeros(acc.shape, F32)
    for b, source, kind in ((0, before, 4), (2, behind, 4 + rows)):
        grads = jnp.concatenate([decoded(gends, kind + h, 1) for h in range(rows)], axis=0).astype(BF16)
        nothing = jnp.zeros((tiles, chans), F32)
        for a in range(3):
            taken = [h + a - 1 for h in range(rows)]
            taken = [source[:, i * chans : (i + 1) * chans] if 0 <= i < rows else nothing for i in taken]
            terms = lax.dot_general(jnp.concatenate(taken, axis=0).astype(BF16), grads, TN, preferred_element_type=F32)
            acc[(3 * a + b) * chans : (3 * a + b + 1) * chans, :] = terms * factor
    mine = piece_of(lax.axis_index("width"), tiles)
    value = total[...] + acc[pl.ds(pl.multiple_of(mine * piece, 16), piece), :]
    power = exponent(value)
    out[:piece, :] = value * jnp.exp2(TOP - power)
    out[piece:, :] = jnp.broadcast_to(power, (POWER, lanes))


def forward_kernel(xs, f, send, keep, acc):
    rows, deep, cols = xs.shape
    groups = lax.axis_size("chan")
    nbits = bits_of(groups)
    block = acc.shape[0] // groups
    me = lax.axis_index("chan")
    for h in range(rows):
        total = None
        for i in range(max(0, h - 1), min(rows, h + 2)):
            part = lax.dot_general(f[i - h + 1], xs[i], TN, preferred_element_type=F32)
            total = part if total is None else total + part
        acc[...] = total
        for q in range(groups):
            owner = me ^ reversed_bits(q, nbits)
            rows_of = acc[pl.ds(pl.multiple_of(owner * block, block), block), :]
            if q < groups // 2:
                keep[q, h] = rows_of
            else:
                send[q - groups // 2, h] = rows_of


def input_kernel(f, ends, *refs):
    groups = lax.axis_size("chan")
    gs, (out, gsc, hsc) = refs[:groups], refs[groups:]
    rows, block, cols = gs[0].shape
    chans = out.shape[1]
    tiles = ends.shape[1]
    lanes = 2 * block
    me, tile = lax.axis_index("chan"), lax.axis_index("width")
    for r in range(groups):
        gsc[:, pl.ds(pl.multiple_of((me ^ r) * block, block), block), :] = gs[r][...]
    for q in range(groups // 2):
        left = ends[(me >> 1) ^ q, jnp.maximum(tile - 1, 0)]
        right = ends[(me >> 1) ^ q, jnp.minimum(tile + 1, tiles - 1)]
        left = jnp.where(tile > 0, left * jnp.exp2(left[1:2] - TOP), 0.0)
        right = jnp.where(tile < tiles - 1, right * jnp.exp2(right[1:2] - TOP), 0.0)
        both = jnp.concatenate([left[4 + rows :], right[4 : 4 + rows], jnp.zeros((16 - 2 * rows, lanes), F32)], axis=0)
        hsc[:, q * lanes : (q + 1) * lanes] = both.astype(BF16)
    lane = lax.broadcasted_iota(jnp.int32, (chans, cols), 1)
    sums = [None] * rows
    for i in range(rows):
        taps = [a for a in range(3) if 0 <= a - 1 + i < rows]
        mats = f[taps[0] * 3 * chans : (taps[-1] + 1) * 3 * chans, :]
        prod = jnp.dot(mats, gsc[i], preferred_element_type=F32)
        sides = lax.dot_general(mats, hsc[...], NT, preferred_element_type=F32)
        for n, a in enumerate(taps):
            h = a - 1 + i
            for b in range(3):
                at = slice((n * 3 + b) * chans, (n * 3 + b + 1) * chans)
                term = prod[at]
                if b == 0:
                    term = jnp.where(lane == cols - 1, sides[at, rows + i : rows + i + 1], pltpu.roll(term, cols - 1, 1))
                elif b == 2:
                    term = jnp.where(lane == 0, sides[at, i : i + 1], pltpu.roll(term, 1, 1))
                sums[h] = term if sums[h] is None else sums[h] + term
    for h in range(rows):
        out[h] = sums[h].astype(BF16)


class Order:
    def __init__(self):
        self.last = None

    def __call__(self, value):
        if self.last is not None:
            value, _ = lax.optimization_barrier((value, self.last))
        self.last = jax.tree.leaves(value)[0]
        return value


def doubled(got, own, late):
    return [jnp.where(late, got, own), jnp.where(late, own, got)]


def in_order(values, late):
    for b, swap in enumerate(late):
        values = [jnp.where(swap, values[n ^ 1 << b], values[n]) for n in range(len(values))]
    return values


def scaled(values, power):
    return (values * jnp.exp2(TOP - power)).astype(F16)


def added(total, got):
    count = total.shape[0]
    return total + got[:count].astype(F32) * jnp.exp2(got[count : count + 1].astype(F32) - TOP)


def chunk_stages(send, keep, finish, order, late, arrived):
    others = 1 << len(late) - 1
    lanes = send.shape[1]
    total, power = keep[:-POWER], keep[-1:]
    piece = total.shape[0] // others

    message = send.astype(F16)
    got = exchange(order(message), "width", 1)
    yield None
    got = order(got)
    yield None
    arrived.append(got[-EDGE:])
    total = added(total, got)
    power = jnp.maximum(power, got[-POWER - EDGE : -POWER - EDGE + 1].astype(F32)) + 1.0
    ends = jnp.concatenate(doubled(got[-EDGE:], message[-EDGE:], late[0]), axis=0)
    tail = jnp.broadcast_to(power, (POWER, lanes)).astype(F16)
    messages = []
    for n in range(1, others):
        part = scaled(total[n * piece : (n + 1) * piece], power)
        messages.append(jnp.concatenate([part, tail, ends], axis=0))
    messages = order(messages)
    gots = [exchange(messages[n - 1], "width", 2 * n) for n in range(1, others)]
    yield None
    gots = order(gots)
    yield None
    total = total[:piece]
    for got in gots:
        total = added(total, got)
    every = in_order([ends] + [got[piece + POWER :] for got in gots], late[1:])
    every = jnp.concatenate([v.reshape(2, EDGE, lanes) for v in every], axis=0).astype(F32)
    own = order(finish(total, every).astype(F16))
    gots = [exchange(own, "width", 2 * n) for n in range(1, others)]
    yield None
    gots = order(gots)
    yield None
    own = order(jnp.stack(in_order([own] + gots, late[1:])))
    got = exchange(own, "width", 1)
    yield None
    got = order(got)
    yield None
    yield jnp.concatenate(doubled(got, own, late[0]), axis=0)


def unpacked(every):
    rows = every.shape[1] - POWER
    scale = jnp.exp2(every[:, rows : rows + 1].astype(F32) - TOP)
    return (every[:, :rows].astype(F32) * scale).reshape(-1, every.shape[2])


def chunk_times(j):
    now = 2.05 * j
    times = [now - 0.1 if j else now]
    for step in range(4):
        now += 2.0
        times += [now - (0.2 if j and step == 0 else 0.1), now]
    return times


def body(activations, filters, cotangent):
    chans, rows, cols = activations.shape
    block = cotangent.shape[0]
    outs = filters.shape[3]
    groups, width = lax.axis_size("chan"), lax.axis_size("width")
    lanes = 2 * block
    late = [((lax.axis_index("width") >> b) & 1) == 1 for b in range(bits_of(width))]
    swaps = [((lax.axis_index("chan") >> b) & 1) == 1 for b in range(1, bits_of(groups))]
    cotangent, late, swaps = lax.optimization_barrier((cotangent, late, swaps))
    mats = jnp.transpose(filters, (1, 2, 0, 3))
    pairs_of_rows = sum(0 <= h + a - 1 < rows for h in range(rows) for a in range(3))
    flops = 2 * pairs_of_rows * 3 * chans * cols * outs
    piece = -(-9 * chans // width)
    piece = -(-piece // 16) * 16
    factor = 1.0 / math.sqrt(rows * cols * width)
    order = Order()
    ends, arrived = {}, []

    def shifted(*sides):
        shapes = [((rows, 3 * chans, cols), BF16), ((2, rows * chans), BF16)]
        return call(taps_kernel, "shifted_taps", shapes, [], 0, activations, *sides)

    def filter_chunk(j):
        send, keep = call(
            functools.partial(filter_kernel, factor, piece, j == 0),
            "filter_terms",
            [((width // 2 * piece + POWER + EDGE, lanes), F32), ((width // 2 * piece + POWER, lanes), F32)],
            [((rows, lanes, cols), BF16), ((width * piece, lanes), F32)],
            flops * 2 // groups,
            bare,
            g[2 * j],
            g[2 * j + 1],
        )

        def finish(total, arrived):
            ends[j] = arrived
            body = functools.partial(border_kernel, factor)
            shape = ((piece + POWER, lanes), F32)
            return call(body, "border_terms", [shape], [((width * piece, lanes), F32)], 0, total, ends[0], ends[j])

        return chunk_stages(send, keep, finish, order, late, arrived)

    def forward():
        odd = late[0]
        pairs = [(i, i + 1) for i in range(1, width - 1, 2)]
        mine = jnp.where(odd, columns[1:2], columns[0:1])
        far = lax.ppermute(order(mine), "width", pairs + [(j, i) for i, j in pairs])
        yield None
        near = arrived[0].astype(F32)
        near = (jnp.where(odd, near[3:4], near[2:3]) * jnp.exp2(near[0:1] - TOP)).astype(BF16)
        far = order(far)
        left, right = jnp.where(odd, near, far), jnp.where(odd, far, near)
        send, keep = call(
            forward_kernel,
            "forward_terms",
            [((groups // 2, rows, block, cols), F32)] * 2,
            [((outs, cols), F32)],
            flops,
            shifted(left, right)[0],
            mats.reshape(3, 3 * chans, outs),
        )
        for b in range(bits_of(groups) - 1):
            got = exchange(order(send), "chan", 1 << b)
            yield None
            total = keep + order(got)
            keep, send = total[: total.shape[0] // 2], total[total.shape[0] // 2 :]
        gots = [exchange(order(send[0, h]), "chan", 1 << bits_of(groups) - 1) for h in range(rows)]
        yield None
        sums = []
        for h in range(rows):
            sums.append((keep[0, h] + order(gots[h])).astype(BF16))
            yield None
        result["conv"] = jnp.transpose(jnp.stack(sums), (1, 0, 2))

    def backward():
        out = call(
            input_kernel,
            "input_terms",
            [((rows, chans, cols), BF16)],
            [((rows, outs, cols), BF16), ((16, outs), BF16)],
            flops,
            mats.reshape(9 * chans, outs),
            jnp.stack([order(ends[j]) for j in range(groups // 2)]),
            *[g[r] for r in range(groups)],
        )
        yield None
        result["grad"] = order(jnp.transpose(out, (1, 0, 2)))

    def chunk(j):
        if j:
            g[2 * j + 1] = order(g[2 * j + 1])
        stages = filter_chunk(j)
        if j == 0:
            next(stages)
            for r in sorted(g):
                if r > 1:
                    g[r | 1] = exchange(order(g[r]), "chan", 1)
            yield None
        for piece in stages:
            pieces[j] = piece
            yield None

    g = {0: order(jnp.transpose(cotangent, (1, 0, 2)))}
    g[1] = exchange(g[0], "chan", 1)
    for b in reversed(range(1, bits_of(groups))):
        for r in [r for r in sorted(g) if r != 1]:
            g[r | 1 << b] = exchange(g[r], "chan", 1 << b)
    bare, columns = shifted()
    pieces, result = {}, {}
    hops = bits_of(groups)
    turns = []
    for j in range(groups // 2):
        stages = chunk(j)
        turns += [(now, stages) for now in chunk_times(j)]
    finale = turns[-1][0]
    conv = forward()
    turns += [(0.1, conv), (2.7, conv)] + [(4.2 + 2 * b, conv) for b in range(hops - 1)]
    turns += [(1.98 + 2 * hops, conv), (3.5 + 2 * hops, conv), (3.6 + 2 * hops, conv)]
    grad = backward()
    turns += [(max(finale - 2.9, chunk_times(groups // 2 - 1)[4] + 0.2), grad), (finale - 0.4, grad)]
    for now, stages in sorted(turns, key=lambda turn: turn[0]):
        next(stages, None)
    conv_output, input_grad = result["conv"], result["grad"]
    pieces = [pieces[j] for j in range(groups // 2)]

    for b in range(bits_of(groups // 2)):
        pieces = [jnp.where(swaps[b], pieces[j ^ 1 << b], pieces[j]) for j in range(len(pieces))]
    grads = jnp.concatenate([unpacked(p) for p in pieces], axis=1)[: 9 * chans]
    grads = jnp.transpose(grads.reshape(3, 3, chans, outs), (2, 0, 1, 3))
    return conv_output, input_grad, grads


def solution(mesh):
    cols = P("chan", None, "width")
    mats = P("chan", None, None, None)
    return jax.shard_map(body, mesh=mesh, in_specs=(cols, mats, cols), out_specs=(cols, cols, mats), check_vma=False)
```

```python
import functools
import math

import jax
import jax.numpy as jnp
from jax import lax
from jax.experimental import pallas as pl
from jax.experimental.pallas import tpu as pltpu
from jax.sharding import PartitionSpec as P

BF16, F16, F32 = jnp.bfloat16, jnp.float16, jnp.float32
LANES = 128
TOP = 14.0
LEAST = 2.0**-110
POWER = 8
EDGE = 8
VMEM = pl.BlockSpec(memory_space=pltpu.VMEM)
NT = (((1,), (1,)), ((), ()))
TN = (((0,), (0,)), ((), ()))


def exchange(value, axis, bit):
    devices = lax.axis_size(axis)
    return lax.ppermute(value, axis, [(i, i ^ bit) for i in range(devices)])


def bits_of(devices):
    return devices.bit_length() - 1


def reversed_bits(index, count):
    out = 0
    for b in range(count):
        out = out + (((index >> b) & 1) << (count - 1 - b))
    return out


def piece_of(tile, tiles):
    return (tile & 1) * (tiles // 2) + (tile >> 1)


def call(body, name, outs, scratch, flops, *args):
    outs = [jax.ShapeDtypeStruct(shape, dtype) for shape, dtype in outs]
    moved = sum(a.size * a.dtype.itemsize for a in list(args) + outs)
    result = pl.pallas_call(
        body,
        out_shape=outs,
        in_specs=[VMEM] * len(args),
        out_specs=[VMEM] * len(outs),
        scratch_shapes=[pltpu.VMEM(shape, dtype) for shape, dtype in scratch],
        compiler_params=pltpu.CompilerParams(vmem_limit_bytes=16 << 20),
        cost_estimate=pl.CostEstimate(flops=flops, bytes_accessed=moved, transcendentals=0),
        name=name,
    )(*args)
    return result[0] if len(outs) == 1 else result


def exponent(values):
    most = jnp.max(jnp.abs(values), axis=(0, 1), keepdims=True)
    return jnp.ceil(jnp.log2(jnp.maximum(most, LEAST)))


def pick_columns(cols):
    row_of = lax.broadcasted_iota(jnp.int32, (16, cols), 0)
    lane = lax.broadcasted_iota(jnp.int32, (16, cols), 1)
    pick = ((row_of == 0) & (lane == 0)) | ((row_of == 1) & (lane == cols - 1))
    return jnp.where(pick, 1.0, 0.0).astype(BF16)


def taps_kernel(x, *refs):
    *sides, out, columns = refs
    chans, rows, cols = x.shape
    row_of = lax.broadcasted_iota(jnp.int32, (16, LANES), 0)
    lane = lax.broadcasted_iota(jnp.int32, (16, LANES), 1)
    place = ((row_of == 0) & (lane == LANES - 1)) | ((row_of == 1) & (lane == 0))
    place = jnp.where(place, 1.0, 0.0).astype(BF16)
    for i in range(rows):
        side = jnp.zeros((chans, LANES), BF16)
        if sides:
            both = [side_ref[...].astype(F32)[:, i * chans : (i + 1) * chans] for side_ref in sides]
            both = jnp.concatenate(both + [jnp.zeros((14, chans), F32)], axis=0).astype(BF16)
            side = lax.dot_general(both, place, TN, preferred_element_type=F32).astype(BF16)
        row = jnp.concatenate([side, x[:, i, :], side], axis=1)
        for b in range(3):
            out[i, b * chans : (b + 1) * chans, :] = row[:, LANES - 1 + b : LANES - 1 + b + cols]
        for at, tile in ((0, x[:, i, :LANES]), (1, x[:, i, cols - LANES :])):
            line = lax.dot_general(pick_columns(LANES), tile, NT, preferred_element_type=F32).astype(BF16)
            columns[at : at + 1, i * chans : (i + 1) * chans] = line[at : at + 1]


def filter_kernel(factor, piece, first, xs, ga, gb, send, keep, gsc, acc):
    rows, deep, cols = xs.shape
    chans = deep // 3
    width = lax.axis_size("width")
    block = ga.shape[1]
    lanes = 2 * block
    parity = lax.axis_index("chan") & 1
    gsc[:, pl.ds(pl.multiple_of(parity * block, block), block), :] = ga[...]
    gsc[:, pl.ds(pl.multiple_of((1 - parity) * block, block), block), :] = gb[...]
    for a in range(3):
        total = None
        for h in range(rows):
            i = h + a - 1
            if 0 <= i < rows:
                part = lax.dot_general(xs[i], gsc[h], NT, preferred_element_type=F32)
                total = part if total is None else total + part
        acc[a * deep : (a + 1) * deep, :] = total * factor
    if acc.shape[0] > 3 * deep:
        acc[3 * deep :, :] = jnp.zeros((acc.shape[0] - 3 * deep, lanes), F32)
    power = exponent(acc[...])
    mine = piece_of(lax.axis_index("width"), width)
    half = width // 2
    for r in range(width):
        rows_of = acc[pl.ds(pl.multiple_of((mine ^ r) * piece, 16), piece), :]
        if r < half:
            keep[r * piece : (r + 1) * piece, :] = rows_of
        else:
            send[(r - half) * piece : (r - half + 1) * piece, :] = rows_of * jnp.exp2(TOP - power)
    power = jnp.broadcast_to(power, (POWER, lanes))
    send[half * piece : half * piece + POWER, :] = power
    keep[half * piece :, :] = power
    pick = pick_columns(cols)
    gends = [lax.dot_general(pick, gsc[h], NT, preferred_element_type=F32) for h in range(rows)]
    gends = jnp.concatenate([gends[h][s : s + 1] for s in range(2) for h in range(rows)], axis=0)
    if first:
        xends = [lax.dot_general(pick, xs[i, chans : 2 * chans], NT, preferred_element_type=F32) for i in range(rows)]
        xends = jnp.concatenate([v[:2] for v in xends], axis=1)
    else:
        xends = jnp.zeros((2, lanes), F32)
    xpower, gpower = exponent(xends), exponent(gends)
    send[half * piece + POWER :, :] = jnp.concatenate(
        [
            jnp.broadcast_to(xpower, (1, lanes)),
            jnp.broadcast_to(gpower, (1, lanes)),
            xends * jnp.exp2(TOP - xpower),
            gends * jnp.exp2(TOP - gpower),
        ],
        axis=0,
    )


def border_kernel(factor, total, xends, gends, out, acc):
    tiles, _, lanes = gends.shape
    piece = total.shape[0]
    rows = 2
    chans = lanes // rows
    tile = lax.broadcasted_iota(jnp.int32, (tiles, lanes), 0)

    def decoded(ref, kind, power):
        return ref[:, kind, :] * jnp.exp2(ref[:, power, :] - TOP)

    before = jnp.where(tile == 0, 0.0, pltpu.roll(decoded(xends, 3, 0), 1, 0))
    behind = jnp.where(tile == tiles - 1, 0.0, pltpu.roll(decoded(xends, 2, 0), tiles - 1, 0))
    acc[...] = jnp.zeros(acc.shape, F32)
    for b, source, kind in ((0, before, 4), (2, behind, 4 + rows)):
        grads = jnp.concatenate([decoded(gends, kind + h, 1) for h in range(rows)], axis=0).astype(BF16)
        nothing = jnp.zeros((tiles, chans), F32)
        for a in range(3):
            taken = [h + a - 1 for h in range(rows)]
            taken = [source[:, i * chans : (i + 1) * chans] if 0 <= i < rows else nothing for i in taken]
            terms = lax.dot_general(jnp.concatenate(taken, axis=0).astype(BF16), grads, TN, preferred_element_type=F32)
            acc[(3 * a + b) * chans : (3 * a + b + 1) * chans, :] = terms * factor
    mine = piece_of(lax.axis_index("width"), tiles)
    value = total[...] + acc[pl.ds(pl.multiple_of(mine * piece, 16), piece), :]
    power = exponent(value)
    out[:piece, :] = value * jnp.exp2(TOP - power)
    out[piece:, :] = jnp.broadcast_to(power, (POWER, lanes))


def place_kernel(piece, layout, *refs):
    *parts, out, sems = refs
    tile, me = lax.axis_index("width"), lax.axis_index("chan") >> 1
    half = lax.axis_size("width") // 2
    lanes = parts[0].shape[1]
    copies = []
    for part, (chunk, other, first) in zip(parts, layout):
        col = pl.multiple_of((me ^ chunk) * lanes, LANES)
        for n in range(part.shape[0] // piece):
            row = ((tile & 1) ^ other) * half + ((tile >> 1) ^ (first + n))
            place = out.at[pl.ds(pl.multiple_of(row * piece, 16), piece), pl.ds(col, lanes)]
            copies.append(pltpu.make_async_copy(part.at[pl.ds(n * piece, piece)], place, sems.at[len(copies)]))
    for copy in copies:
        copy.start()
    for copy in copies:
        copy.wait()


def forward_kernel(xs, f, send, keep, acc):
    rows, deep, cols = xs.shape
    groups = lax.axis_size("chan")
    nbits = bits_of(groups)
    block = acc.shape[0] // groups
    me = lax.axis_index("chan")
    for h in range(rows):
        total = None
        for i in range(max(0, h - 1), min(rows, h + 2)):
            part = lax.dot_general(f[i - h + 1], xs[i], TN, preferred_element_type=F32)
            total = part if total is None else total + part
        acc[...] = total
        for q in range(groups):
            owner = me ^ reversed_bits(q, nbits)
            rows_of = acc[pl.ds(pl.multiple_of(owner * block, block), block), :]
            if q < groups // 2:
                keep[q, h] = rows_of
            else:
                send[q - groups // 2, h] = rows_of


def input_kernel(f, ends, *refs):
    groups = lax.axis_size("chan")
    gs, (out, gsc, hsc) = refs[:groups], refs[groups:]
    rows, block, cols = gs[0].shape
    chans = out.shape[1]
    tiles = ends.shape[1]
    lanes = 2 * block
    me, tile = lax.axis_index("chan"), lax.axis_index("width")
    for r in range(groups):
        gsc[:, pl.ds(pl.multiple_of((me ^ r) * block, block), block), :] = gs[r][...]
    for q in range(groups // 2):
        left = ends[(me >> 1) ^ q, jnp.maximum(tile - 1, 0)]
        right = ends[(me >> 1) ^ q, jnp.minimum(tile + 1, tiles - 1)]
        left = jnp.where(tile > 0, left * jnp.exp2(left[1:2] - TOP), 0.0)
        right = jnp.where(tile < tiles - 1, right * jnp.exp2(right[1:2] - TOP), 0.0)
        both = jnp.concatenate([left[4 + rows :], right[4 : 4 + rows], jnp.zeros((16 - 2 * rows, lanes), F32)], axis=0)
        hsc[:, q * lanes : (q + 1) * lanes] = both.astype(BF16)
    lane = lax.broadcasted_iota(jnp.int32, (chans, cols), 1)
    sums = [None] * rows
    for i in range(rows):
        taps = [a for a in range(3) if 0 <= a - 1 + i < rows]
        mats = f[taps[0] * 3 * chans : (taps[-1] + 1) * 3 * chans, :]
        prod = jnp.dot(mats, gsc[i], preferred_element_type=F32)
        sides = lax.dot_general(mats, hsc[...], NT, preferred_element_type=F32)
        for n, a in enumerate(taps):
            h = a - 1 + i
            for b in range(3):
                at = slice((n * 3 + b) * chans, (n * 3 + b + 1) * chans)
                term = prod[at]
                if b == 0:
                    term = jnp.where(lane == cols - 1, sides[at, rows + i : rows + i + 1], pltpu.roll(term, cols - 1, 1))
                elif b == 2:
                    term = jnp.where(lane == 0, sides[at, i : i + 1], pltpu.roll(term, 1, 1))
                sums[h] = term if sums[h] is None else sums[h] + term
    for h in range(rows):
        out[h] = sums[h].astype(BF16)


class Order:
    def __init__(self):
        self.last = None

    def __call__(self, value):
        if self.last is not None:
            value, _ = lax.optimization_barrier((value, self.last))
        self.last = jax.tree.leaves(value)[0]
        return value


def doubled(got, own, late):
    return [jnp.where(late, got, own), jnp.where(late, own, got)]


def in_order(values, late):
    for b, swap in enumerate(late):
        values = [jnp.where(swap, values[n ^ 1 << b], values[n]) for n in range(len(values))]
    return values


def scaled(values, power):
    return (values * jnp.exp2(TOP - power)).astype(F16)


def added(total, got):
    count = total.shape[0]
    return total + got[:count].astype(F32) * jnp.exp2(got[count : count + 1].astype(F32) - TOP)


def chunk_stages(send, keep, finish, order, late, direct, halves, arrived):
    others = 1 << len(late) - 1
    lanes = send.shape[1]
    total, power = keep[:-POWER], keep[-1:]
    piece = total.shape[0] // others

    message = send.astype(F16)
    got = exchange(order(message), "width", 1)
    yield None
    got = order(got)
    yield None
    arrived.append(got[-EDGE:])
    total = added(total, got)
    power = jnp.maximum(power, got[-POWER - EDGE : -POWER - EDGE + 1].astype(F32)) + 1.0
    ends = jnp.concatenate(doubled(got[-EDGE:], message[-EDGE:], late[0]), axis=0)
    tail = jnp.broadcast_to(power, (POWER, lanes)).astype(F16)
    messages = []
    for n in range(1, others):
        part = scaled(total[n * piece : (n + 1) * piece], power)
        messages.append(jnp.concatenate([part, tail, ends], axis=0))
    messages = order(messages)
    gots = [exchange(messages[n - 1], "width", 2 * n) for n in range(1, others)]
    yield None
    gots = order(gots)
    yield None
    total = total[:piece]
    for got in gots:
        total = added(total, got)
    every = in_order([ends] + [got[piece + POWER :] for got in gots], late[1:])
    every = jnp.concatenate([v.reshape(2, EDGE, lanes) for v in every], axis=0).astype(F32)
    own = order(finish(total, every).astype(F16))
    own = [own]
    if direct:
        own += [exchange(own[0], "width", 2 * n) for n in range(1, others)]
        yield None
    else:
        for b in reversed(range(1, len(late))):
            got = exchange(jnp.stack(own), "width", 1 << b)
            yield None
            got = order(got)
            yield None
            own = order([piece for piece in own] + [got[n] for n in range(len(own))])
        own = [own[reversed_bits(n, len(late) - 1)] for n in range(others)]
    parts = (range(others // 2), range(others // 2, others)) if direct and halves else (range(others),)
    gots = []
    for part in parts:
        part = order([own[n] for n in part])
        yield None
        part = order(jnp.stack(part))
        gots.append((part, exchange(part, "width", 1)))
    pairs = []
    for part, got in gots:
        yield None
        pairs.append((unpacked(part), unpacked(order(got))))
    yield pairs


def unpacked(every):
    rows = every.shape[1] - POWER
    scale = jnp.exp2(every[:, rows : rows + 1].astype(F32) - TOP)
    return (every[:, :rows].astype(F32) * scale).reshape(-1, every.shape[2])


FIRST = (0.0, 1.9, 2.0, 3.9, 4.0, 5.9, 6.0, 7.9)
LATER = (1.95, 3.85, 4.05, 5.95, 6.05, 6.5, 6.6, 6.7, 9.9, 10.0)
FORWARD = (0.1, 0.2, 2.7, 4.2, 5.98, 6.75)
BACKWARD = (6.72, 9.6)
PARTNERS = 0.3
AFTER = 2.0
DIRECT = (True, True)
SPLIT = True
HALVES = (False, True)


def chunk_times(j, steps):
    base = FIRST if j == 0 else [now + AFTER * (j - 1) for now in LATER]
    if DIRECT[min(j, 1)]:
        return base
    hops = []
    for n in range(1, steps):
        now = base[4] + (base[6] - base[4]) * n / (steps - 1)
        hops += [now - 0.1 if n < steps - 1 else base[5], now]
    return [*base[:5], *hops, *base[7:]]


def body(activations, filters, cotangent):
    chans, rows, cols = activations.shape
    block = cotangent.shape[0]
    outs = filters.shape[3]
    groups, width = lax.axis_size("chan"), lax.axis_size("width")
    lanes = 2 * block
    late = [((lax.axis_index("width") >> b) & 1) == 1 for b in range(bits_of(width))]
    swaps = [((lax.axis_index("chan") >> b) & 1) == 1 for b in range(1, bits_of(groups))]
    cotangent, late, swaps = lax.optimization_barrier((cotangent, late, swaps))
    mats = jnp.transpose(filters, (1, 2, 0, 3))
    pairs_of_rows = sum(0 <= h + a - 1 < rows for h in range(rows) for a in range(3))
    flops = 2 * pairs_of_rows * 3 * chans * cols * outs
    piece = -(-9 * chans // width)
    piece = -(-piece // 16) * 16
    factor = 1.0 / math.sqrt(rows * cols * width)
    order = Order()
    ends, arrived = {}, []

    def shifted(*sides):
        shapes = [((rows, 3 * chans, cols), BF16), ((2, rows * chans), BF16)]
        return call(taps_kernel, "shifted_taps", shapes, [], 0, activations, *sides)

    def filter_chunk(j):
        send, keep = call(
            functools.partial(filter_kernel, factor, piece, j == 0),
            "filter_terms",
            [((width // 2 * piece + POWER + EDGE, lanes), F32), ((width // 2 * piece + POWER, lanes), F32)],
            [((rows, lanes, cols), BF16), ((width * piece, lanes), F32)],
            flops * 2 // groups,
            bare,
            g[2 * j],
            g[2 * j + 1],
        )

        def finish(total, arrived):
            ends[j] = arrived
            body = functools.partial(border_kernel, factor)
            shape = ((piece + POWER, lanes), F32)
            return call(body, "border_terms", [shape], [((width * piece, lanes), F32)], 0, total, ends[0], ends[j])

        return chunk_stages(send, keep, finish, order, late, DIRECT[min(j, 1)], HALVES[min(j, 1)], arrived)

    def forward():
        odd = late[0]
        pairs = [(i, i + 1) for i in range(1, width - 1, 2)]
        mine = jnp.where(odd, columns[1:2], columns[0:1])
        far = lax.ppermute(order(mine), "width", pairs + [(j, i) for i, j in pairs])
        yield None
        far = order(far)
        yield None
        near = order(arrived[0]).astype(F32)
        near = (jnp.where(odd, near[3:4], near[2:3]) * jnp.exp2(near[0:1] - TOP)).astype(BF16)
        left, right = jnp.where(odd, near, far), jnp.where(odd, far, near)
        send, keep = call(
            forward_kernel,
            "forward_terms",
            [((groups // 2, rows, block, cols), F32)] * 2,
            [((outs, cols), F32)],
            flops,
            shifted(left, right)[0],
            mats.reshape(3, 3 * chans, outs),
        )
        for b in range(bits_of(groups) - 1):
            got = exchange(order(send), "chan", 1 << b)
            yield None
            total = keep + order(got)
            keep, send = total[: total.shape[0] // 2], total[total.shape[0] // 2 :]
        hop = 1 << bits_of(groups) - 1
        gots = [exchange(order(send[0, h]), "chan", hop) for h in range(rows)] if SPLIT else []
        sums = []
        for h in range(rows):
            got = gots[h] if SPLIT else exchange(order(send[0, h]), "chan", hop)
            yield None
            sums.append((keep[0, h] + order(got)).astype(BF16))
        result["conv"] = jnp.transpose(jnp.stack(sums), (1, 0, 2))

    def backward():
        out = call(
            input_kernel,
            "input_terms",
            [((rows, chans, cols), BF16)],
            [((rows, outs, cols), BF16), ((16, outs), BF16)],
            flops,
            mats.reshape(9 * chans, outs),
            jnp.stack([order(ends[j]) for j in range(groups // 2)]),
            *[g[r] for r in range(groups)],
        )
        yield None
        result["grad"] = order(jnp.transpose(out, (1, 0, 2)))

    def chunk(j):
        if j:
            g[2 * j + 1] = order(g[2 * j + 1])
        stages = filter_chunk(j)
        for piece in stages:
            pieces[j] = piece
            yield None

    def partners():
        for r in sorted(g):
            if r > 1:
                g[r | 1] = exchange(order(g[r]), "chan", 1)
        yield None

    g = {0: order(jnp.transpose(cotangent, (1, 0, 2)))}
    g[1] = exchange(g[0], "chan", 1)
    for b in reversed(range(1, bits_of(groups))):
        for r in [r for r in sorted(g) if r != 1]:
            g[r | 1 << b] = exchange(g[r], "chan", 1 << b)
    bare, columns = shifted()
    pieces, result = {}, {}
    hops = bits_of(groups)
    turns = []
    for j in range(groups // 2):
        stages = chunk(j)
        turns += [(now, stages) for now in chunk_times(j, bits_of(width))]
    conv = forward()
    extra = AFTER * (groups // 2 - 2)
    turns += [(FORWARD[0], conv), (FORWARD[1], conv), (PARTNERS, partners()), (FORWARD[2], conv)]
    turns += [(FORWARD[3] + b, conv) for b in range(hops - 1)]
    turns += [(FORWARD[4] + hops - 2, conv), (FORWARD[5] + hops - 2, conv), (FORWARD[5] + hops - 1.99, conv)]
    grad = backward()
    turns += [(BACKWARD[0] + extra, grad), (BACKWARD[1] + extra, grad)]
    for now, stages in sorted(turns, key=lambda turn: turn[0]):
        next(stages, None)
    for stages in dict.fromkeys(stages for _, stages in turns):
        for _ in stages:
            pass
    conv_output, input_grad = result["conv"], result["grad"]
    pieces = [pieces[j] for j in range(groups // 2)]

    if lanes % LANES:
        sides = [[jnp.concatenate([pair[side] for pair in pieces[j]], axis=0) for side in range(2)] for j in range(len(pieces))]
        sides = [[jnp.split(v, width // 2, axis=0) for v in pair] for pair in sides]
        sides = [[jnp.concatenate(in_order(v, late[1:]), axis=0) for v in pair] for pair in sides]
        pieces = [jnp.concatenate(doubled(got, own, late[0]), axis=0) for own, got in sides]
        for b in range(bits_of(groups // 2)):
            pieces = [jnp.where(swaps[b], pieces[j ^ 1 << b], pieces[j]) for j in range(len(pieces))]
        grads = jnp.concatenate(pieces, axis=1)
    else:
        parts, layout = [], []
        for j, pairs in enumerate(pieces):
            first = 0
            for own, got in pairs:
                parts += [own, got]
                layout += [(j, 0, first), (j, 1, first)]
                first += own.shape[0] // piece
        grads = pl.pallas_call(
            functools.partial(place_kernel, piece, layout),
            out_shape=jax.ShapeDtypeStruct((width * piece, outs), F32),
            in_specs=[VMEM] * len(parts),
            out_specs=pl.BlockSpec(memory_space=pl.ANY),
            scratch_shapes=[pltpu.SemaphoreType.DMA((width * groups // 2,))],
            compiler_params=pltpu.CompilerParams(vmem_limit_bytes=16 << 20),
            name="place_pieces",
        )(*parts)
    grads = grads[: 9 * chans]
    grads = jnp.transpose(grads.reshape(3, 3, chans, outs), (2, 0, 1, 3))
    return conv_output, input_grad, grads


def solution(mesh):
    cols = P("chan", None, "width")
    mats = P("chan", None, None, None)
    return jax.shard_map(body, mesh=mesh, in_specs=(cols, mats, cols), out_specs=(cols, cols, mats), check_vma=False)
```

```python
import functools
import math

import jax
import jax.numpy as jnp
from jax import lax
from jax.experimental import pallas as pl
from jax.experimental.pallas import tpu as pltpu
from jax.sharding import PartitionSpec as P

BF16, F16, F32 = jnp.bfloat16, jnp.float16, jnp.float32
LANES = 128
TOP = 14.0
LEAST = 2.0**-110
POWER = 8
EDGE = 8
VMEM = pl.BlockSpec(memory_space=pltpu.VMEM)
NT = (((1,), (1,)), ((), ()))
TN = (((0,), (0,)), ((), ()))


def exchange(value, axis, bit):
    devices = lax.axis_size(axis)
    return lax.ppermute(value, axis, [(i, i ^ bit) for i in range(devices)])


def bits_of(devices):
    return devices.bit_length() - 1


def reversed_bits(index, count):
    out = 0
    for b in range(count):
        out = out + (((index >> b) & 1) << (count - 1 - b))
    return out


def piece_of(tile, tiles):
    return (tile & 1) * (tiles // 2) + (tile >> 1)


def call(body, name, outs, scratch, flops, *args):
    outs = [jax.ShapeDtypeStruct(shape, dtype) for shape, dtype in outs]
    moved = sum(a.size * a.dtype.itemsize for a in list(args) + outs)
    result = pl.pallas_call(
        body,
        out_shape=outs,
        in_specs=[VMEM] * len(args),
        out_specs=[VMEM] * len(outs),
        scratch_shapes=[pltpu.VMEM(shape, dtype) for shape, dtype in scratch],
        compiler_params=pltpu.CompilerParams(vmem_limit_bytes=16 << 20),
        cost_estimate=pl.CostEstimate(flops=flops, bytes_accessed=moved, transcendentals=0),
        name=name,
    )(*args)
    return result[0] if len(outs) == 1 else result


def exponent(values):
    most = jnp.max(jnp.abs(values), axis=(0, 1), keepdims=True)
    return jnp.ceil(jnp.log2(jnp.maximum(most, LEAST)))


def pick_columns(cols):
    row_of = lax.broadcasted_iota(jnp.int32, (16, cols), 0)
    lane = lax.broadcasted_iota(jnp.int32, (16, cols), 1)
    pick = ((row_of == 0) & (lane == 0)) | ((row_of == 1) & (lane == cols - 1))
    return jnp.where(pick, 1.0, 0.0).astype(BF16)


def taps_kernel(x, *refs):
    *sides, out, columns = refs
    chans, rows, cols = x.shape
    row_of = lax.broadcasted_iota(jnp.int32, (16, LANES), 0)
    lane = lax.broadcasted_iota(jnp.int32, (16, LANES), 1)
    place = ((row_of == 0) & (lane == LANES - 1)) | ((row_of == 1) & (lane == 0))
    place = jnp.where(place, 1.0, 0.0).astype(BF16)
    for i in range(rows):
        side = jnp.zeros((chans, LANES), BF16)
        if sides:
            both = [side_ref[...].astype(F32)[:, i * chans : (i + 1) * chans] for side_ref in sides]
            both = jnp.concatenate(both + [jnp.zeros((14, chans), F32)], axis=0).astype(BF16)
            side = lax.dot_general(both, place, TN, preferred_element_type=F32).astype(BF16)
        row = jnp.concatenate([side, x[:, i, :], side], axis=1)
        for b in range(3):
            out[i, b * chans : (b + 1) * chans, :] = row[:, LANES - 1 + b : LANES - 1 + b + cols]
        for at, tile in ((0, x[:, i, :LANES]), (1, x[:, i, cols - LANES :])):
            line = lax.dot_general(pick_columns(LANES), tile, NT, preferred_element_type=F32).astype(BF16)
            columns[at : at + 1, i * chans : (i + 1) * chans] = line[at : at + 1]


def filter_kernel(factor, piece, first, xs, ga, gb, send, keep, gsc, acc):
    rows, deep, cols = xs.shape
    chans = deep // 3
    width = lax.axis_size("width")
    block = ga.shape[1]
    lanes = 2 * block
    parity = lax.axis_index("chan") & 1
    gsc[:, pl.ds(pl.multiple_of(parity * block, block), block), :] = ga[...]
    gsc[:, pl.ds(pl.multiple_of((1 - parity) * block, block), block), :] = gb[...]
    for a in range(3):
        total = None
        for h in range(rows):
            i = h + a - 1
            if 0 <= i < rows:
                part = lax.dot_general(xs[i], gsc[h], NT, preferred_element_type=F32)
                total = part if total is None else total + part
        acc[a * deep : (a + 1) * deep, :] = total * factor
    if acc.shape[0] > 3 * deep:
        acc[3 * deep :, :] = jnp.zeros((acc.shape[0] - 3 * deep, lanes), F32)
    power = exponent(acc[...])
    mine = piece_of(lax.axis_index("width"), width)
    half = width // 2
    for r in range(width):
        rows_of = acc[pl.ds(pl.multiple_of((mine ^ r) * piece, 16), piece), :]
        if r < half:
            keep[r * piece : (r + 1) * piece, :] = rows_of
        else:
            send[(r - half) * piece : (r - half + 1) * piece, :] = rows_of * jnp.exp2(TOP - power)
    power = jnp.broadcast_to(power, (POWER, lanes))
    send[half * piece : half * piece + POWER, :] = power
    keep[half * piece :, :] = power
    pick = pick_columns(cols)
    gends = [lax.dot_general(pick, gsc[h], NT, preferred_element_type=F32) for h in range(rows)]
    gends = jnp.concatenate([gends[h][s : s + 1] for s in range(2) for h in range(rows)], axis=0)
    if first:
        xends = [lax.dot_general(pick, xs[i, chans : 2 * chans], NT, preferred_element_type=F32) for i in range(rows)]
        xends = jnp.concatenate([v[:2] for v in xends], axis=1)
    else:
        xends = jnp.zeros((2, lanes), F32)
    xpower, gpower = exponent(xends), exponent(gends)
    send[half * piece + POWER :, :] = jnp.concatenate(
        [
            jnp.broadcast_to(xpower, (1, lanes)),
            jnp.broadcast_to(gpower, (1, lanes)),
            xends * jnp.exp2(TOP - xpower),
            gends * jnp.exp2(TOP - gpower),
        ],
        axis=0,
    )


def border_kernel(factor, total, xends, gends, out, acc):
    tiles, _, lanes = gends.shape
    piece = total.shape[0]
    rows = 2
    chans = lanes // rows
    tile = lax.broadcasted_iota(jnp.int32, (tiles, lanes), 0)

    def decoded(ref, kind, power):
        return ref[:, kind, :] * jnp.exp2(ref[:, power, :] - TOP)

    before = jnp.where(tile == 0, 0.0, pltpu.roll(decoded(xends, 3, 0), 1, 0))
    behind = jnp.where(tile == tiles - 1, 0.0, pltpu.roll(decoded(xends, 2, 0), tiles - 1, 0))
    acc[...] = jnp.zeros(acc.shape, F32)
    for b, source, kind in ((0, before, 4), (2, behind, 4 + rows)):
        grads = jnp.concatenate([decoded(gends, kind + h, 1) for h in range(rows)], axis=0).astype(BF16)
        nothing = jnp.zeros((tiles, chans), F32)
        for a in range(3):
            taken = [h + a - 1 for h in range(rows)]
            taken = [source[:, i * chans : (i + 1) * chans] if 0 <= i < rows else nothing for i in taken]
            terms = lax.dot_general(jnp.concatenate(taken, axis=0).astype(BF16), grads, TN, preferred_element_type=F32)
            acc[(3 * a + b) * chans : (3 * a + b + 1) * chans, :] = terms * factor
    mine = piece_of(lax.axis_index("width"), tiles)
    value = total[...] + acc[pl.ds(pl.multiple_of(mine * piece, 16), piece), :]
    power = exponent(value)
    out[:piece, :] = value * jnp.exp2(TOP - power)
    out[piece:, :] = jnp.broadcast_to(power, (POWER, lanes))


def place_kernel(piece, layout, *refs):
    *parts, out, sems = refs
    tile, me = lax.axis_index("width"), lax.axis_index("chan") >> 1
    half = lax.axis_size("width") // 2
    lanes = parts[0].shape[1]
    copies = []
    for part, (chunk, other, first) in zip(parts, layout):
        col = pl.multiple_of((me ^ chunk) * lanes, LANES)
        for n in range(part.shape[0] // piece):
            row = ((tile & 1) ^ other) * half + ((tile >> 1) ^ (first + n))
            place = out.at[pl.ds(pl.multiple_of(row * piece, 16), piece), pl.ds(col, lanes)]
            copies.append(pltpu.make_async_copy(part.at[pl.ds(n * piece, piece)], place, sems.at[len(copies)]))
    for copy in copies:
        copy.start()
    for copy in copies:
        copy.wait()


def forward_kernel(xs, f, send, keep, acc):
    rows, deep, cols = xs.shape
    groups = lax.axis_size("chan")
    nbits = bits_of(groups)
    block = acc.shape[0] // groups
    me = lax.axis_index("chan")
    for h in range(rows):
        total = None
        for i in range(max(0, h - 1), min(rows, h + 2)):
            part = lax.dot_general(f[i - h + 1], xs[i], TN, preferred_element_type=F32)
            total = part if total is None else total + part
        acc[...] = total
        for q in range(groups):
            owner = me ^ reversed_bits(q, nbits)
            rows_of = acc[pl.ds(pl.multiple_of(owner * block, block), block), :]
            if q < groups // 2:
                keep[q, h] = rows_of
            else:
                send[q - groups // 2, h] = rows_of


def input_kernel(f, ends, *refs):
    groups = lax.axis_size("chan")
    gs, (out, gsc, hsc) = refs[:groups], refs[groups:]
    rows, block, cols = gs[0].shape
    chans = out.shape[1]
    tiles = ends.shape[1]
    lanes = 2 * block
    me, tile = lax.axis_index("chan"), lax.axis_index("width")
    for r in range(groups):
        gsc[:, pl.ds(pl.multiple_of((me ^ r) * block, block), block), :] = gs[r][...]
    for q in range(groups // 2):
        left = ends[(me >> 1) ^ q, jnp.maximum(tile - 1, 0)]
        right = ends[(me >> 1) ^ q, jnp.minimum(tile + 1, tiles - 1)]
        left = jnp.where(tile > 0, left * jnp.exp2(left[1:2] - TOP), 0.0)
        right = jnp.where(tile < tiles - 1, right * jnp.exp2(right[1:2] - TOP), 0.0)
        both = jnp.concatenate([left[4 + rows :], right[4 : 4 + rows], jnp.zeros((16 - 2 * rows, lanes), F32)], axis=0)
        hsc[:, q * lanes : (q + 1) * lanes] = both.astype(BF16)
    lane = lax.broadcasted_iota(jnp.int32, (chans, cols), 1)
    sums = [None] * rows
    for i in range(rows):
        taps = [a for a in range(3) if 0 <= a - 1 + i < rows]
        mats = f[taps[0] * 3 * chans : (taps[-1] + 1) * 3 * chans, :]
        prod = jnp.dot(mats, gsc[i], preferred_element_type=F32)
        sides = lax.dot_general(mats, hsc[...], NT, preferred_element_type=F32)
        for n, a in enumerate(taps):
            h = a - 1 + i
            for b in range(3):
                at = slice((n * 3 + b) * chans, (n * 3 + b + 1) * chans)
                term = prod[at]
                if b == 0:
                    term = jnp.where(lane == cols - 1, sides[at, rows + i : rows + i + 1], pltpu.roll(term, cols - 1, 1))
                elif b == 2:
                    term = jnp.where(lane == 0, sides[at, i : i + 1], pltpu.roll(term, 1, 1))
                sums[h] = term if sums[h] is None else sums[h] + term
    for h in range(rows):
        out[h] = sums[h].astype(BF16)


class Order:
    def __init__(self):
        self.last = None

    def __call__(self, value):
        if self.last is not None:
            value, _ = lax.optimization_barrier((value, self.last))
        self.last = jax.tree.leaves(value)[0]
        return value


def doubled(got, own, late):
    return [jnp.where(late, got, own), jnp.where(late, own, got)]


def in_order(values, late):
    for b, swap in enumerate(late):
        values = [jnp.where(swap, values[n ^ 1 << b], values[n]) for n in range(len(values))]
    return values


def scaled(values, power):
    return (values * jnp.exp2(TOP - power)).astype(F16)


def added(total, got):
    count = total.shape[0]
    return total + got[:count].astype(F32) * jnp.exp2(got[count : count + 1].astype(F32) - TOP)


def chunk_stages(send, keep, finish, order, late, direct, halves, arrived):
    others = 1 << len(late) - 1
    lanes = send.shape[1]
    total, power = keep[:-POWER], keep[-1:]
    piece = total.shape[0] // others

    message = send.astype(F16)
    got = exchange(order(message), "width", 1)
    yield None
    got = order(got)
    yield None
    arrived.append(got[-EDGE:])
    total = added(total, got)
    power = jnp.maximum(power, got[-POWER - EDGE : -POWER - EDGE + 1].astype(F32)) + 1.0
    ends = jnp.concatenate(doubled(got[-EDGE:], message[-EDGE:], late[0]), axis=0)
    tail = jnp.broadcast_to(power, (POWER, lanes)).astype(F16)
    messages = []
    for n in range(1, others):
        part = scaled(total[n * piece : (n + 1) * piece], power)
        messages.append(jnp.concatenate([part, tail, ends], axis=0))
    messages = order(messages)
    gots = [exchange(messages[n - 1], "width", 2 * n) for n in range(1, others)]
    yield None
    gots = order(gots)
    yield None
    total = total[:piece]
    for got in gots:
        total = added(total, got)
    every = in_order([ends] + [got[piece + POWER :] for got in gots], late[1:])
    every = jnp.concatenate([v.reshape(2, EDGE, lanes) for v in every], axis=0).astype(F32)
    own = order(finish(total, every).astype(F16))
    own = [own]
    if direct:
        own += [exchange(own[0], "width", 2 * n) for n in range(1, others)]
        yield None
    else:
        for b in reversed(range(1, len(late))):
            got = exchange(jnp.stack(own), "width", 1 << b)
            yield None
            got = order(got)
            yield None
            own = order([piece for piece in own] + [got[n] for n in range(len(own))])
        own = [own[reversed_bits(n, len(late) - 1)] for n in range(others)]
    parts = (range(others // 2), range(others // 2, others)) if direct and halves else (range(others),)
    gots = []
    for part in parts:
        part = order([own[n] for n in part])
        yield None
        part = order(jnp.stack(part))
        gots.append((part, exchange(part, "width", 1)))
    pairs = []
    for part, got in gots:
        yield None
        pairs.append((unpacked(part), unpacked(order(got))))
    yield pairs


def unpacked(every):
    rows = every.shape[1] - POWER
    scale = jnp.exp2(every[:, rows : rows + 1].astype(F32) - TOP)
    return (every[:, :rows].astype(F32) * scale).reshape(-1, every.shape[2])


FIRST = (0.0, 1.9, 2.0, 3.9, 4.0, 5.9, 6.0, 7.9)
LATER = (1.95, 3.85, 4.05, 5.95, 6.05, 6.5, 6.6, 6.7, 9.9, 10.0)
FORWARD = (0.1, 0.2, 2.7, 4.03, 5.94, 6.45)
BACKWARD = (6.72, 9.6)
PARTNERS = 0.3
AFTER = 2.0
DIRECT = (True, True)
SPLIT = True
HALVES = (False, True)


def chunk_times(j, steps):
    base = FIRST if j == 0 else [now + AFTER * (j - 1) for now in LATER]
    if DIRECT[min(j, 1)]:
        return base
    hops = []
    for n in range(1, steps):
        now = base[4] + (base[6] - base[4]) * n / (steps - 1)
        hops += [now - 0.1 if n < steps - 1 else base[5], now]
    return [*base[:5], *hops, *base[7:]]


def body(activations, filters, cotangent):
    chans, rows, cols = activations.shape
    block = cotangent.shape[0]
    outs = filters.shape[3]
    groups, width = lax.axis_size("chan"), lax.axis_size("width")
    lanes = 2 * block
    late = [((lax.axis_index("width") >> b) & 1) == 1 for b in range(bits_of(width))]
    swaps = [((lax.axis_index("chan") >> b) & 1) == 1 for b in range(1, bits_of(groups))]
    cotangent, late, swaps = lax.optimization_barrier((cotangent, late, swaps))
    mats = jnp.transpose(filters, (1, 2, 0, 3))
    pairs_of_rows = sum(0 <= h + a - 1 < rows for h in range(rows) for a in range(3))
    flops = 2 * pairs_of_rows * 3 * chans * cols * outs
    piece = -(-9 * chans // width)
    piece = -(-piece // 16) * 16
    factor = 1.0 / math.sqrt(rows * cols * width)
    order = Order()
    ends, arrived = {}, []

    def shifted(*sides):
        shapes = [((rows, 3 * chans, cols), BF16), ((2, rows * chans), BF16)]
        return call(taps_kernel, "shifted_taps", shapes, [], 0, activations, *sides)

    def filter_chunk(j):
        send, keep = call(
            functools.partial(filter_kernel, factor, piece, j == 0),
            "filter_terms",
            [((width // 2 * piece + POWER + EDGE, lanes), F32), ((width // 2 * piece + POWER, lanes), F32)],
            [((rows, lanes, cols), BF16), ((width * piece, lanes), F32)],
            flops * 2 // groups,
            bare,
            g[2 * j],
            g[2 * j + 1],
        )

        def finish(total, arrived):
            ends[j] = arrived
            body = functools.partial(border_kernel, factor)
            shape = ((piece + POWER, lanes), F32)
            return call(body, "border_terms", [shape], [((width * piece, lanes), F32)], 0, total, ends[0], ends[j])

        return chunk_stages(send, keep, finish, order, late, DIRECT[min(j, 1)], HALVES[min(j, 1)], arrived)

    def forward():
        odd = late[0]
        pairs = [(i, i + 1) for i in range(1, width - 1, 2)]
        mine = jnp.where(odd, columns[1:2], columns[0:1])
        far = lax.ppermute(order(mine), "width", pairs + [(j, i) for i, j in pairs])
        yield None
        far = order(far)
        yield None
        near = order(arrived[0]).astype(F32)
        near = (jnp.where(odd, near[3:4], near[2:3]) * jnp.exp2(near[0:1] - TOP)).astype(BF16)
        left, right = jnp.where(odd, near, far), jnp.where(odd, far, near)
        send, keep = call(
            forward_kernel,
            "forward_terms",
            [((groups // 2, rows, block, cols), F32)] * 2,
            [((outs, cols), F32)],
            flops,
            shifted(left, right)[0],
            mats.reshape(3, 3 * chans, outs),
        )
        for b in range(bits_of(groups) - 1):
            got = exchange(order(send), "chan", 1 << b)
            yield None
            total = keep + order(got)
            keep, send = total[: total.shape[0] // 2], total[total.shape[0] // 2 :]
        hop = 1 << bits_of(groups) - 1
        gots = [exchange(order(send[0, h]), "chan", hop) for h in range(rows)] if SPLIT else []
        sums = []
        for h in range(rows):
            got = gots[h] if SPLIT else exchange(order(send[0, h]), "chan", hop)
            yield None
            sums.append((keep[0, h] + order(got)).astype(BF16))
        result["conv"] = jnp.transpose(jnp.stack(sums), (1, 0, 2))

    def backward():
        out = call(
            input_kernel,
            "input_terms",
            [((rows, chans, cols), BF16)],
            [((rows, outs, cols), BF16), ((16, outs), BF16)],
            flops,
            mats.reshape(9 * chans, outs),
            jnp.stack([order(ends[j]) for j in range(groups // 2)]),
            *[g[r] for r in range(groups)],
        )
        yield None
        result["grad"] = order(jnp.transpose(out, (1, 0, 2)))

    def chunk(j):
        if j:
            g[2 * j + 1] = order(g[2 * j + 1])
        stages = filter_chunk(j)
        for piece in stages:
            pieces[j] = piece
            yield None

    def partners():
        for r in sorted(g):
            if r > 1:
                g[r | 1] = exchange(order(g[r]), "chan", 1)
        yield None

    g = {0: order(jnp.transpose(cotangent, (1, 0, 2)))}
    g[1] = exchange(g[0], "chan", 1)
    for b in reversed(range(1, bits_of(groups))):
        for r in [r for r in sorted(g) if r != 1]:
            g[r | 1 << b] = exchange(g[r], "chan", 1 << b)
    bare, columns = shifted()
    pieces, result = {}, {}
    hops = bits_of(groups)
    turns = []
    for j in range(groups // 2):
        stages = chunk(j)
        turns += [(now, stages) for now in chunk_times(j, bits_of(width))]
    conv = forward()
    extra = AFTER * (groups // 2 - 2)
    turns += [(FORWARD[0], conv), (FORWARD[1], conv), (PARTNERS, partners()), (FORWARD[2], conv)]
    turns += [(FORWARD[3] + b, conv) for b in range(hops - 1)]
    turns += [(FORWARD[4] + hops - 2, conv), (FORWARD[5] + hops - 2, conv), (FORWARD[5] + hops - 1.99, conv)]
    grad = backward()
    turns += [(BACKWARD[0] + extra, grad), (BACKWARD[1] + extra, grad)]
    for now, stages in sorted(turns, key=lambda turn: turn[0]):
        next(stages, None)
    for stages in dict.fromkeys(stages for _, stages in turns):
        for _ in stages:
            pass
    conv_output, input_grad = result["conv"], result["grad"]
    pieces = [pieces[j] for j in range(groups // 2)]

    if lanes % LANES:
        sides = [[jnp.concatenate([pair[side] for pair in pieces[j]], axis=0) for side in range(2)] for j in range(len(pieces))]
        sides = [[jnp.split(v, width // 2, axis=0) for v in pair] for pair in sides]
        sides = [[jnp.concatenate(in_order(v, late[1:]), axis=0) for v in pair] for pair in sides]
        pieces = [jnp.concatenate(doubled(got, own, late[0]), axis=0) for own, got in sides]
        for b in range(bits_of(groups // 2)):
            pieces = [jnp.where(swaps[b], pieces[j ^ 1 << b], pieces[j]) for j in range(len(pieces))]
        grads = jnp.concatenate(pieces, axis=1)
    else:
        parts, layout = [], []
        for j, pairs in enumerate(pieces):
            first = 0
            for own, got in pairs:
                parts += [own, got]
                layout += [(j, 0, first), (j, 1, first)]
                first += own.shape[0] // piece
        grads = pl.pallas_call(
            functools.partial(place_kernel, piece, layout),
            out_shape=jax.ShapeDtypeStruct((width * piece, outs), F32),
            in_specs=[VMEM] * len(parts),
            out_specs=pl.BlockSpec(memory_space=pl.ANY),
            scratch_shapes=[pltpu.SemaphoreType.DMA((width * groups // 2,))],
            compiler_params=pltpu.CompilerParams(vmem_limit_bytes=16 << 20),
            name="place_pieces",
        )(*parts)
    grads = grads[: 9 * chans]
    grads = jnp.transpose(grads.reshape(3, 3, chans, outs), (2, 0, 1, 3))
    return conv_output, input_grad, grads


def solution(mesh):
    cols = P("chan", None, "width")
    mats = P("chan", None, None, None)
    return jax.shard_map(body, mesh=mesh, in_specs=(cols, mats, cols), out_specs=(cols, cols, mats), check_vma=False)
```

```python
import functools
import math

import jax
import jax.numpy as jnp
from jax import lax
from jax.experimental import pallas as pl
from jax.experimental.pallas import tpu as pltpu
from jax.sharding import PartitionSpec as P

BF16, F16, F32 = jnp.bfloat16, jnp.float16, jnp.float32
LANES = 128
TOP = 14.0
LEAST = 2.0**-110
POWER = 8
EDGE = 8
VMEM = pl.BlockSpec(memory_space=pltpu.VMEM)
NT = (((1,), (1,)), ((), ()))
TN = (((0,), (0,)), ((), ()))


def exchange(value, axis, bit):
    devices = lax.axis_size(axis)
    return lax.ppermute(value, axis, [(i, i ^ bit) for i in range(devices)])


def bits_of(devices):
    return devices.bit_length() - 1


def reversed_bits(index, count):
    out = 0
    for b in range(count):
        out = out + (((index >> b) & 1) << (count - 1 - b))
    return out


def piece_of(tile, tiles):
    return (tile & 1) * (tiles // 2) + (tile >> 1)


def call(body, name, outs, scratch, flops, *args):
    outs = [jax.ShapeDtypeStruct(shape, dtype) for shape, dtype in outs]
    moved = sum(a.size * a.dtype.itemsize for a in list(args) + outs)
    result = pl.pallas_call(
        body,
        out_shape=outs,
        in_specs=[VMEM] * len(args),
        out_specs=[VMEM] * len(outs),
        scratch_shapes=[pltpu.VMEM(shape, dtype) for shape, dtype in scratch],
        compiler_params=pltpu.CompilerParams(vmem_limit_bytes=16 << 20),
        cost_estimate=pl.CostEstimate(flops=flops, bytes_accessed=moved, transcendentals=0),
        name=name,
    )(*args)
    return result[0] if len(outs) == 1 else result


def exponent(values):
    most = jnp.max(jnp.abs(values), axis=(0, 1), keepdims=True)
    return jnp.ceil(jnp.log2(jnp.maximum(most, LEAST)))


def pick_columns(cols):
    row_of = lax.broadcasted_iota(jnp.int32, (16, cols), 0)
    lane = lax.broadcasted_iota(jnp.int32, (16, cols), 1)
    pick = ((row_of == 0) & (lane == 0)) | ((row_of == 1) & (lane == cols - 1))
    return jnp.where(pick, 1.0, 0.0).astype(BF16)


def taps_kernel(x, *refs):
    *sides, out, columns = refs
    chans, rows, cols = x.shape
    row_of = lax.broadcasted_iota(jnp.int32, (16, LANES), 0)
    lane = lax.broadcasted_iota(jnp.int32, (16, LANES), 1)
    place = ((row_of == 0) & (lane == LANES - 1)) | ((row_of == 1) & (lane == 0))
    place = jnp.where(place, 1.0, 0.0).astype(BF16)
    for i in range(rows):
        side = jnp.zeros((chans, LANES), BF16)
        if sides:
            both = [side_ref[...].astype(F32)[:, i * chans : (i + 1) * chans] for side_ref in sides]
            both = jnp.concatenate(both + [jnp.zeros((14, chans), F32)], axis=0).astype(BF16)
            side = lax.dot_general(both, place, TN, preferred_element_type=F32).astype(BF16)
        row = jnp.concatenate([side, x[:, i, :], side], axis=1)
        for b in range(3):
            out[i, b * chans : (b + 1) * chans, :] = row[:, LANES - 1 + b : LANES - 1 + b + cols]
        for at, tile in ((0, x[:, i, :LANES]), (1, x[:, i, cols - LANES :])):
            line = lax.dot_general(pick_columns(LANES), tile, NT, preferred_element_type=F32).astype(BF16)
            columns[at : at + 1, i * chans : (i + 1) * chans] = line[at : at + 1]


def filter_kernel(factor, piece, first, xs, ga, gb, send, keep, gsc, acc):
    rows, deep, cols = xs.shape
    chans = deep // 3
    width = lax.axis_size("width")
    block = ga.shape[1]
    lanes = 2 * block
    parity = lax.axis_index("chan") & 1
    gsc[:, pl.ds(pl.multiple_of(parity * block, block), block), :] = ga[...]
    gsc[:, pl.ds(pl.multiple_of((1 - parity) * block, block), block), :] = gb[...]
    for a in range(3):
        total = None
        for h in range(rows):
            i = h + a - 1
            if 0 <= i < rows:
                part = lax.dot_general(xs[i], gsc[h], NT, preferred_element_type=F32)
                total = part if total is None else total + part
        acc[a * deep : (a + 1) * deep, :] = total * factor
    if acc.shape[0] > 3 * deep:
        acc[3 * deep :, :] = jnp.zeros((acc.shape[0] - 3 * deep, lanes), F32)
    power = exponent(acc[...])
    mine = piece_of(lax.axis_index("width"), width)
    half = width // 2
    for r in range(width):
        rows_of = acc[pl.ds(pl.multiple_of((mine ^ r) * piece, 16), piece), :]
        if r < half:
            keep[r * piece : (r + 1) * piece, :] = rows_of
        else:
            send[(r - half) * piece : (r - half + 1) * piece, :] = rows_of * jnp.exp2(TOP - power)
    power = jnp.broadcast_to(power, (POWER, lanes))
    send[half * piece : half * piece + POWER, :] = power
    keep[half * piece :, :] = power
    pick = pick_columns(cols)
    gends = [lax.dot_general(pick, gsc[h], NT, preferred_element_type=F32) for h in range(rows)]
    gends = jnp.concatenate([gends[h][s : s + 1] for s in range(2) for h in range(rows)], axis=0)
    if first:
        xends = [lax.dot_general(pick, xs[i, chans : 2 * chans], NT, preferred_element_type=F32) for i in range(rows)]
        xends = jnp.concatenate([v[:2] for v in xends], axis=1)
    else:
        xends = jnp.zeros((2, lanes), F32)
    xpower, gpower = exponent(xends), exponent(gends)
    send[half * piece + POWER :, :] = jnp.concatenate(
        [
            jnp.broadcast_to(xpower, (1, lanes)),
            jnp.broadcast_to(gpower, (1, lanes)),
            xends * jnp.exp2(TOP - xpower),
            gends * jnp.exp2(TOP - gpower),
        ],
        axis=0,
    )


def border_kernel(factor, total, xends, gends, out, acc):
    tiles, _, lanes = gends.shape
    piece = total.shape[0]
    rows = 2
    chans = lanes // rows
    tile = lax.broadcasted_iota(jnp.int32, (tiles, lanes), 0)

    def decoded(ref, kind, power):
        return ref[:, kind, :] * jnp.exp2(ref[:, power, :] - TOP)

    before = jnp.where(tile == 0, 0.0, pltpu.roll(decoded(xends, 3, 0), 1, 0))
    behind = jnp.where(tile == tiles - 1, 0.0, pltpu.roll(decoded(xends, 2, 0), tiles - 1, 0))
    acc[...] = jnp.zeros(acc.shape, F32)
    for b, source, kind in ((0, before, 4), (2, behind, 4 + rows)):
        grads = jnp.concatenate([decoded(gends, kind + h, 1) for h in range(rows)], axis=0).astype(BF16)
        nothing = jnp.zeros((tiles, chans), F32)
        for a in range(3):
            taken = [h + a - 1 for h in range(rows)]
            taken = [source[:, i * chans : (i + 1) * chans] if 0 <= i < rows else nothing for i in taken]
            terms = lax.dot_general(jnp.concatenate(taken, axis=0).astype(BF16), grads, TN, preferred_element_type=F32)
            acc[(3 * a + b) * chans : (3 * a + b + 1) * chans, :] = terms * factor
    mine = piece_of(lax.axis_index("width"), tiles)
    value = total[...] + acc[pl.ds(pl.multiple_of(mine * piece, 16), piece), :]
    power = exponent(value)
    out[:piece, :] = value * jnp.exp2(TOP - power)
    out[piece:, :] = jnp.broadcast_to(power, (POWER, lanes))


def place_kernel(piece, layout, *refs):
    *parts, out, sems = refs
    tile, me = lax.axis_index("width"), lax.axis_index("chan") >> 1
    tiles = lax.axis_size("width")
    lanes = parts[0].shape[1]
    copies = []
    for part, (chunk, owners) in zip(parts, layout):
        col = pl.multiple_of((me ^ chunk) * lanes, LANES)
        for n, owner in enumerate(owners):
            row = pl.multiple_of(piece_of(tile ^ owner, tiles) * piece, 16)
            place = out.at[pl.ds(row, piece), pl.ds(col, lanes)]
            copies.append(pltpu.make_async_copy(part.at[pl.ds(n * piece, piece)], place, sems.at[len(copies)]))
    for copy in copies:
        copy.start()
    for copy in copies:
        copy.wait()


def forward_kernel(xs, f, send, keep, acc):
    rows, deep, cols = xs.shape
    groups = lax.axis_size("chan")
    nbits = bits_of(groups)
    block = acc.shape[0] // groups
    me = lax.axis_index("chan")
    for h in range(rows):
        total = None
        for i in range(max(0, h - 1), min(rows, h + 2)):
            part = lax.dot_general(f[i - h + 1], xs[i], TN, preferred_element_type=F32)
            total = part if total is None else total + part
        acc[...] = total
        for q in range(groups):
            owner = me ^ reversed_bits(q, nbits)
            rows_of = acc[pl.ds(pl.multiple_of(owner * block, block), block), :]
            if q < groups // 2:
                keep[q, h] = rows_of
            else:
                send[q - groups // 2, h] = rows_of


def input_kernel(f, ends, *refs):
    groups = lax.axis_size("chan")
    gs, (out, gsc, hsc) = refs[:groups], refs[groups:]
    rows, block, cols = gs[0].shape
    chans = out.shape[1]
    tiles = ends.shape[1]
    lanes = 2 * block
    me, tile = lax.axis_index("chan"), lax.axis_index("width")
    for r in range(groups):
        gsc[:, pl.ds(pl.multiple_of((me ^ r) * block, block), block), :] = gs[r][...]
    for q in range(groups // 2):
        left = ends[(me >> 1) ^ q, jnp.maximum(tile - 1, 0)]
        right = ends[(me >> 1) ^ q, jnp.minimum(tile + 1, tiles - 1)]
        left = jnp.where(tile > 0, left * jnp.exp2(left[1:2] - TOP), 0.0)
        right = jnp.where(tile < tiles - 1, right * jnp.exp2(right[1:2] - TOP), 0.0)
        both = jnp.concatenate([left[4 + rows :], right[4 : 4 + rows], jnp.zeros((16 - 2 * rows, lanes), F32)], axis=0)
        hsc[:, q * lanes : (q + 1) * lanes] = both.astype(BF16)
    lane = lax.broadcasted_iota(jnp.int32, (chans, cols), 1)
    sums = [None] * rows
    for i in range(rows):
        taps = [a for a in range(3) if 0 <= a - 1 + i < rows]
        mats = f[taps[0] * 3 * chans : (taps[-1] + 1) * 3 * chans, :]
        prod = jnp.dot(mats, gsc[i], preferred_element_type=F32)
        sides = lax.dot_general(mats, hsc[...], NT, preferred_element_type=F32)
        for n, a in enumerate(taps):
            h = a - 1 + i
            for b in range(3):
                at = slice((n * 3 + b) * chans, (n * 3 + b + 1) * chans)
                term = prod[at]
                if b == 0:
                    term = jnp.where(lane == cols - 1, sides[at, rows + i : rows + i + 1], pltpu.roll(term, cols - 1, 1))
                elif b == 2:
                    term = jnp.where(lane == 0, sides[at, i : i + 1], pltpu.roll(term, 1, 1))
                sums[h] = term if sums[h] is None else sums[h] + term
    for h in range(rows):
        out[h] = sums[h].astype(BF16)


class Order:
    def __init__(self):
        self.last = None

    def __call__(self, value):
        if self.last is not None:
            value, _ = lax.optimization_barrier((value, self.last))
        self.last = jax.tree.leaves(value)[0]
        return value


def doubled(got, own, late):
    return [jnp.where(late, got, own), jnp.where(late, own, got)]


def in_order(values, late):
    for b, swap in enumerate(late):
        values = [jnp.where(swap, values[n ^ 1 << b], values[n]) for n in range(len(values))]
    return values


def scaled(values, power):
    return (values * jnp.exp2(TOP - power)).astype(F16)


def added(total, got):
    count = total.shape[0]
    return total + got[:count].astype(F32) * jnp.exp2(got[count : count + 1].astype(F32) - TOP)


def chunk_stages(send, keep, finish, order, late, direct, halves, arrived):
    others = 1 << len(late) - 1
    lanes = send.shape[1]
    total, power = keep[:-POWER], keep[-1:]
    piece = total.shape[0] // others

    message = send.astype(F16)
    got = exchange(order(message), "width", 1)
    yield None
    got = order(got)
    yield None
    arrived.append(got[-EDGE:])
    total = added(total, got)
    power = jnp.maximum(power, got[-POWER - EDGE : -POWER - EDGE + 1].astype(F32)) + 1.0
    ends = jnp.concatenate(doubled(got[-EDGE:], message[-EDGE:], late[0]), axis=0)
    tail = jnp.broadcast_to(power, (POWER, lanes)).astype(F16)
    messages = []
    for n in range(1, others):
        part = scaled(total[n * piece : (n + 1) * piece], power)
        messages.append(jnp.concatenate([part, tail, ends], axis=0))
    messages = order(messages)
    gots = [exchange(messages[n - 1], "width", 2 * n) for n in range(1, others)]
    yield None
    gots = order(gots)
    yield None
    total = total[:piece]
    for got in gots:
        total = added(total, got)
    every = in_order([ends] + [got[piece + POWER :] for got in gots], late[1:])
    every = jnp.concatenate([v.reshape(2, EDGE, lanes) for v in every], axis=0).astype(F32)
    own = order(finish(total, every).astype(F16))
    if not direct:
        own = own[None]
        bits = [*reversed(range(2, len(late))), 0, 1]
        tiles = [0]
        for b in bits:
            got = exchange(own, "width", 1 << b)
            yield None
            got = order(got)
            yield None
            own = order(jnp.concatenate([own, got], axis=0))
            tiles += [tile ^ 1 << b for tile in tiles]
        yield [(unpacked(own), tiles)]
        return
    own = [own] + [exchange(own, "width", 2 * n) for n in range(1, others)]
    yield None
    gots = []
    for part in (range(others // 2), range(others // 2, others)) if halves else (range(others),):
        tiles = [2 * n for n in part]
        part = order([own[n] for n in part])
        yield None
        part = order(jnp.stack(part))
        gots.append((part, exchange(part, "width", 1), tiles))
    parts = []
    for part, got, tiles in gots:
        yield None
        parts += [(unpacked(part), tiles), (unpacked(order(got)), [tile ^ 1 for tile in tiles])]
    yield parts


def unpacked(every):
    rows = every.shape[1] - POWER
    scale = jnp.exp2(every[:, rows : rows + 1].astype(F32) - TOP)
    return (every[:, :rows].astype(F32) * scale).reshape(-1, every.shape[2])


FIRST = (0.0, 1.9, 2.0, 3.9, 4.0, 4.6, 4.62, 5.5, 5.52, 7.9)
LATER = (1.95, 3.85, 4.05, 5.95, 6.05, 6.5, 6.6, 6.7, 9.9, 10.0)
FORWARD = (0.1, 0.2, 2.7, 4.03, 5.94, 6.45)
BACKWARD = (6.72, 9.6)
PARTNERS = 0.3
AFTER = 2.0
DIRECT = (False, True)
SPLIT = True
HALVES = (False, True)


def chunk_times(j, steps):
    base = FIRST if j == 0 else [now + AFTER * (j - 1) for now in LATER]
    return base


def body(activations, filters, cotangent):
    chans, rows, cols = activations.shape
    block = cotangent.shape[0]
    outs = filters.shape[3]
    groups, width = lax.axis_size("chan"), lax.axis_size("width")
    lanes = 2 * block
    late = [((lax.axis_index("width") >> b) & 1) == 1 for b in range(bits_of(width))]
    swaps = [((lax.axis_index("chan") >> b) & 1) == 1 for b in range(1, bits_of(groups))]
    cotangent, late, swaps = lax.optimization_barrier((cotangent, late, swaps))
    mats = jnp.transpose(filters, (1, 2, 0, 3))
    pairs_of_rows = sum(0 <= h + a - 1 < rows for h in range(rows) for a in range(3))
    flops = 2 * pairs_of_rows * 3 * chans * cols * outs
    piece = -(-9 * chans // width)
    piece = -(-piece // 16) * 16
    factor = 1.0 / math.sqrt(rows * cols * width)
    order = Order()
    ends, arrived = {}, []

    def shifted(*sides):
        shapes = [((rows, 3 * chans, cols), BF16), ((2, rows * chans), BF16)]
        return call(taps_kernel, "shifted_taps", shapes, [], 0, activations, *sides)

    def filter_chunk(j):
        send, keep = call(
            functools.partial(filter_kernel, factor, piece, j == 0),
            "filter_terms",
            [((width // 2 * piece + POWER + EDGE, lanes), F32), ((width // 2 * piece + POWER, lanes), F32)],
            [((rows, lanes, cols), BF16), ((width * piece, lanes), F32)],
            flops * 2 // groups,
            bare,
            g[2 * j],
            g[2 * j + 1],
        )

        def finish(total, arrived):
            ends[j] = arrived
            body = functools.partial(border_kernel, factor)
            shape = ((piece + POWER, lanes), F32)
            return call(body, "border_terms", [shape], [((width * piece, lanes), F32)], 0, total, ends[0], ends[j])

        return chunk_stages(send, keep, finish, order, late, DIRECT[min(j, 1)], HALVES[min(j, 1)], arrived)

    def forward():
        odd = late[0]
        pairs = [(i, i + 1) for i in range(1, width - 1, 2)]
        mine = jnp.where(odd, columns[1:2], columns[0:1])
        far = lax.ppermute(order(mine), "width", pairs + [(j, i) for i, j in pairs])
        yield None
        far = order(far)
        yield None
        near = order(arrived[0]).astype(F32)
        near = (jnp.where(odd, near[3:4], near[2:3]) * jnp.exp2(near[0:1] - TOP)).astype(BF16)
        left, right = jnp.where(odd, near, far), jnp.where(odd, far, near)
        send, keep = call(
            forward_kernel,
            "forward_terms",
            [((groups // 2, rows, block, cols), F32)] * 2,
            [((outs, cols), F32)],
            flops,
            shifted(left, right)[0],
            mats.reshape(3, 3 * chans, outs),
        )
        for b in range(bits_of(groups) - 1):
            got = exchange(order(send), "chan", 1 << b)
            yield None
            total = keep + order(got)
            keep, send = total[: total.shape[0] // 2], total[total.shape[0] // 2 :]
        hop = 1 << bits_of(groups) - 1
        gots = [exchange(order(send[0, h]), "chan", hop) for h in range(rows)] if SPLIT else []
        sums = []
        for h in range(rows):
            got = gots[h] if SPLIT else exchange(order(send[0, h]), "chan", hop)
            yield None
            sums.append((keep[0, h] + order(got)).astype(BF16))
        result["conv"] = jnp.transpose(jnp.stack(sums), (1, 0, 2))

    def backward():
        out = call(
            input_kernel,
            "input_terms",
            [((rows, chans, cols), BF16)],
            [((rows, outs, cols), BF16), ((16, outs), BF16)],
            flops,
            mats.reshape(9 * chans, outs),
            jnp.stack([order(ends[j]) for j in range(groups // 2)]),
            *[g[r] for r in range(groups)],
        )
        yield None
        result["grad"] = order(jnp.transpose(out, (1, 0, 2)))

    def chunk(j):
        if j:
            g[2 * j + 1] = order(g[2 * j + 1])
        stages = filter_chunk(j)
        for piece in stages:
            pieces[j] = piece
            yield None

    def partners():
        for r in sorted(g):
            if r > 1:
                g[r | 1] = exchange(order(g[r]), "chan", 1)
        yield None

    g = {0: order(jnp.transpose(cotangent, (1, 0, 2)))}
    g[1] = exchange(g[0], "chan", 1)
    for b in reversed(range(1, bits_of(groups))):
        for r in [r for r in sorted(g) if r != 1]:
            g[r | 1 << b] = exchange(g[r], "chan", 1 << b)
    bare, columns = shifted()
    pieces, result = {}, {}
    hops = bits_of(groups)
    turns = []
    for j in range(groups // 2):
        stages = chunk(j)
        turns += [(now, stages) for now in chunk_times(j, bits_of(width))]
    conv = forward()
    extra = AFTER * (groups // 2 - 2)
    turns += [(FORWARD[0], conv), (FORWARD[1], conv), (PARTNERS, partners()), (FORWARD[2], conv)]
    turns += [(FORWARD[3] + b, conv) for b in range(hops - 1)]
    turns += [(FORWARD[4] + hops - 2, conv), (FORWARD[5] + hops - 2, conv), (FORWARD[5] + hops - 1.99, conv)]
    grad = backward()
    turns += [(BACKWARD[0] + extra, grad), (BACKWARD[1] + extra, grad)]
    for now, stages in sorted(turns, key=lambda turn: turn[0]):
        next(stages, None)
    for stages in dict.fromkeys(stages for _, stages in turns):
        for _ in stages:
            pass
    conv_output, input_grad = result["conv"], result["grad"]
    pieces = [pieces[j] for j in range(groups // 2)]

    if lanes % LANES:
        for j in range(len(pieces)):
            terms = {}
            for part, owners in pieces[j]:
                terms.update(zip(owners, jnp.split(part, len(owners), axis=0)))
            terms = in_order([terms[n] for n in range(width)], late)
            pieces[j] = jnp.concatenate([terms[p // (width // 2) + 2 * (p % (width // 2))] for p in range(width)], axis=0)
        for b in range(bits_of(groups // 2)):
            pieces = [jnp.where(swaps[b], pieces[j ^ 1 << b], pieces[j]) for j in range(len(pieces))]
        grads = jnp.concatenate(pieces, axis=1)
    else:
        parts = [part for chunk in pieces for part, _ in chunk]
        layout = [(j, owners) for j, chunk in enumerate(pieces) for _, owners in chunk]
        grads = pl.pallas_call(
            functools.partial(place_kernel, piece, layout),
            out_shape=jax.ShapeDtypeStruct((width * piece, outs), F32),
            in_specs=[VMEM] * len(parts),
            out_specs=pl.BlockSpec(memory_space=pl.ANY),
            scratch_shapes=[pltpu.SemaphoreType.DMA((width * groups // 2,))],
            compiler_params=pltpu.CompilerParams(vmem_limit_bytes=16 << 20),
            name="place_pieces",
        )(*parts)
    grads = grads[: 9 * chans]
    grads = jnp.transpose(grads.reshape(3, 3, chans, outs), (2, 0, 1, 3))
    return conv_output, input_grad, grads


def solution(mesh):
    cols = P("chan", None, "width")
    mats = P("chan", None, None, None)
    return jax.shard_map(body, mesh=mesh, in_specs=(cols, mats, cols), out_specs=(cols, cols, mats), check_vma=False)
```

```python
import functools
import math

import jax
import jax.numpy as jnp
from jax import lax
from jax.experimental import pallas as pl
from jax.experimental.pallas import tpu as pltpu
from jax.sharding import PartitionSpec as P

BF16, F16, F32 = jnp.bfloat16, jnp.float16, jnp.float32
LANES = 128
TOP = 14.0
LEAST = 2.0**-110
POWER = 8
EDGE = 8
VMEM = pl.BlockSpec(memory_space=pltpu.VMEM)
NT = (((1,), (1,)), ((), ()))
TN = (((0,), (0,)), ((), ()))


def exchange(value, axis, bit):
    devices = lax.axis_size(axis)
    return lax.ppermute(value, axis, [(i, i ^ bit) for i in range(devices)])


def bits_of(devices):
    return devices.bit_length() - 1


def reversed_bits(index, count):
    out = 0
    for b in range(count):
        out = out + (((index >> b) & 1) << (count - 1 - b))
    return out


def piece_of(tile, tiles):
    return (tile & 1) * (tiles // 2) + (tile >> 1)


def call(body, name, outs, scratch, flops, *args):
    outs = [jax.ShapeDtypeStruct(shape, dtype) for shape, dtype in outs]
    moved = sum(a.size * a.dtype.itemsize for a in list(args) + outs)
    result = pl.pallas_call(
        body,
        out_shape=outs,
        in_specs=[VMEM] * len(args),
        out_specs=[VMEM] * len(outs),
        scratch_shapes=[pltpu.VMEM(shape, dtype) for shape, dtype in scratch],
        compiler_params=pltpu.CompilerParams(vmem_limit_bytes=16 << 20),
        cost_estimate=pl.CostEstimate(flops=flops, bytes_accessed=moved, transcendentals=0),
        name=name,
    )(*args)
    return result[0] if len(outs) == 1 else result


def exponent(values):
    most = jnp.max(jnp.abs(values), axis=(0, 1), keepdims=True)
    return jnp.ceil(jnp.log2(jnp.maximum(most, LEAST)))


def pick_columns(cols):
    row_of = lax.broadcasted_iota(jnp.int32, (16, cols), 0)
    lane = lax.broadcasted_iota(jnp.int32, (16, cols), 1)
    pick = ((row_of == 0) & (lane == 0)) | ((row_of == 1) & (lane == cols - 1))
    return jnp.where(pick, 1.0, 0.0).astype(BF16)


def taps_kernel(x, *refs):
    *sides, out, columns = refs
    chans, rows, cols = x.shape
    row_of = lax.broadcasted_iota(jnp.int32, (16, LANES), 0)
    lane = lax.broadcasted_iota(jnp.int32, (16, LANES), 1)
    place = ((row_of == 0) & (lane == LANES - 1)) | ((row_of == 1) & (lane == 0))
    place = jnp.where(place, 1.0, 0.0).astype(BF16)
    for i in range(rows):
        side = jnp.zeros((chans, LANES), BF16)
        if sides:
            both = [side_ref[...].astype(F32)[:, i * chans : (i + 1) * chans] for side_ref in sides]
            both = jnp.concatenate(both + [jnp.zeros((14, chans), F32)], axis=0).astype(BF16)
            side = lax.dot_general(both, place, TN, preferred_element_type=F32).astype(BF16)
        row = jnp.concatenate([side, x[:, i, :], side], axis=1)
        for b in range(3):
            out[i, b * chans : (b + 1) * chans, :] = row[:, LANES - 1 + b : LANES - 1 + b + cols]
        for at, tile in ((0, x[:, i, :LANES]), (1, x[:, i, cols - LANES :])):
            line = lax.dot_general(pick_columns(LANES), tile, NT, preferred_element_type=F32).astype(BF16)
            columns[at : at + 1, i * chans : (i + 1) * chans] = line[at : at + 1]


def filter_kernel(factor, piece, first, xs, ga, gb, send, keep, gsc, acc):
    rows, deep, cols = xs.shape
    chans = deep // 3
    width = lax.axis_size("width")
    block = ga.shape[1]
    lanes = 2 * block
    parity = lax.axis_index("chan") & 1
    gsc[:, pl.ds(pl.multiple_of(parity * block, block), block), :] = ga[...]
    gsc[:, pl.ds(pl.multiple_of((1 - parity) * block, block), block), :] = gb[...]
    for a in range(3):
        total = None
        for h in range(rows):
            i = h + a - 1
            if 0 <= i < rows:
                part = lax.dot_general(xs[i], gsc[h], NT, preferred_element_type=F32)
                total = part if total is None else total + part
        acc[a * deep : (a + 1) * deep, :] = total * factor
    if acc.shape[0] > 3 * deep:
        acc[3 * deep :, :] = jnp.zeros((acc.shape[0] - 3 * deep, lanes), F32)
    power = exponent(acc[...])
    mine = piece_of(lax.axis_index("width"), width)
    half = width // 2
    for r in range(width):
        rows_of = acc[pl.ds(pl.multiple_of((mine ^ r) * piece, 16), piece), :]
        if r < half:
            keep[r * piece : (r + 1) * piece, :] = rows_of
        else:
            send[(r - half) * piece : (r - half + 1) * piece, :] = rows_of * jnp.exp2(TOP - power)
    power = jnp.broadcast_to(power, (POWER, lanes))
    send[half * piece : half * piece + POWER, :] = power
    keep[half * piece :, :] = power
    pick = pick_columns(cols)
    gends = [lax.dot_general(pick, gsc[h], NT, preferred_element_type=F32) for h in range(rows)]
    gends = jnp.concatenate([gends[h][s : s + 1] for s in range(2) for h in range(rows)], axis=0)
    if first:
        xends = [lax.dot_general(pick, xs[i, chans : 2 * chans], NT, preferred_element_type=F32) for i in range(rows)]
        xends = jnp.concatenate([v[:2] for v in xends], axis=1)
    else:
        xends = jnp.zeros((2, lanes), F32)
    xpower, gpower = exponent(xends), exponent(gends)
    send[half * piece + POWER :, :] = jnp.concatenate(
        [
            jnp.broadcast_to(xpower, (1, lanes)),
            jnp.broadcast_to(gpower, (1, lanes)),
            xends * jnp.exp2(TOP - xpower),
            gends * jnp.exp2(TOP - gpower),
        ],
        axis=0,
    )


def border_kernel(factor, total, xends, gends, out, acc):
    tiles, _, lanes = gends.shape
    piece = total.shape[0]
    rows = 2
    chans = lanes // rows
    tile = lax.broadcasted_iota(jnp.int32, (tiles, lanes), 0)

    def decoded(ref, kind, power):
        return ref[:, kind, :] * jnp.exp2(ref[:, power, :] - TOP)

    before = jnp.where(tile == 0, 0.0, pltpu.roll(decoded(xends, 3, 0), 1, 0))
    behind = jnp.where(tile == tiles - 1, 0.0, pltpu.roll(decoded(xends, 2, 0), tiles - 1, 0))
    acc[...] = jnp.zeros(acc.shape, F32)
    for b, source, kind in ((0, before, 4), (2, behind, 4 + rows)):
        grads = jnp.concatenate([decoded(gends, kind + h, 1) for h in range(rows)], axis=0).astype(BF16)
        nothing = jnp.zeros((tiles, chans), F32)
        for a in range(3):
            taken = [h + a - 1 for h in range(rows)]
            taken = [source[:, i * chans : (i + 1) * chans] if 0 <= i < rows else nothing for i in taken]
            terms = lax.dot_general(jnp.concatenate(taken, axis=0).astype(BF16), grads, TN, preferred_element_type=F32)
            acc[(3 * a + b) * chans : (3 * a + b + 1) * chans, :] = terms * factor
    mine = piece_of(lax.axis_index("width"), tiles)
    value = total[...] + acc[pl.ds(pl.multiple_of(mine * piece, 16), piece), :]
    power = exponent(value)
    out[:piece, :] = value * jnp.exp2(TOP - power)
    out[piece:, :] = jnp.broadcast_to(power, (POWER, lanes))


def place_kernel(piece, layout, *refs):
    *parts, out, sems = refs
    tile, me = lax.axis_index("width"), lax.axis_index("chan") >> 1
    tiles = lax.axis_size("width")
    lanes = parts[0].shape[1]
    copies = []
    for part, (chunk, owners) in zip(parts, layout):
        col = pl.multiple_of((me ^ chunk) * lanes, LANES)
        for n, owner in enumerate(owners):
            row = pl.multiple_of(piece_of(tile ^ owner, tiles) * piece, 16)
            place = out.at[pl.ds(row, piece), pl.ds(col, lanes)]
            copies.append(pltpu.make_async_copy(part.at[pl.ds(n * piece, piece)], place, sems.at[len(copies)]))
    for copy in copies:
        copy.start()
    for copy in copies:
        copy.wait()


def forward_kernel(xs, f, send, keep, acc):
    rows, deep, cols = xs.shape
    groups = lax.axis_size("chan")
    nbits = bits_of(groups)
    block = acc.shape[0] // groups
    me = lax.axis_index("chan")
    for h in range(rows):
        total = None
        for i in range(max(0, h - 1), min(rows, h + 2)):
            part = lax.dot_general(f[i - h + 1], xs[i], TN, preferred_element_type=F32)
            total = part if total is None else total + part
        acc[...] = total
        for q in range(groups):
            owner = me ^ reversed_bits(q, nbits)
            rows_of = acc[pl.ds(pl.multiple_of(owner * block, block), block), :]
            if q < groups // 2:
                keep[q, h] = rows_of
            else:
                send[q - groups // 2, h] = rows_of


def input_kernel(f, ends, *refs):
    groups = lax.axis_size("chan")
    gs, (out, gsc, hsc) = refs[:groups], refs[groups:]
    rows, block, cols = gs[0].shape
    chans = out.shape[1]
    tiles = ends.shape[1]
    lanes = 2 * block
    me, tile = lax.axis_index("chan"), lax.axis_index("width")
    for r in range(groups):
        gsc[:, pl.ds(pl.multiple_of((me ^ r) * block, block), block), :] = gs[r][...]
    for q in range(groups // 2):
        left = ends[(me >> 1) ^ q, jnp.maximum(tile - 1, 0)]
        right = ends[(me >> 1) ^ q, jnp.minimum(tile + 1, tiles - 1)]
        left = jnp.where(tile > 0, left * jnp.exp2(left[1:2] - TOP), 0.0)
        right = jnp.where(tile < tiles - 1, right * jnp.exp2(right[1:2] - TOP), 0.0)
        both = jnp.concatenate([left[4 + rows :], right[4 : 4 + rows], jnp.zeros((16 - 2 * rows, lanes), F32)], axis=0)
        hsc[:, q * lanes : (q + 1) * lanes] = both.astype(BF16)
    lane = lax.broadcasted_iota(jnp.int32, (chans, cols), 1)
    sums = [None] * rows
    for i in range(rows):
        taps = [a for a in range(3) if 0 <= a - 1 + i < rows]
        mats = f[taps[0] * 3 * chans : (taps[-1] + 1) * 3 * chans, :]
        prod = jnp.dot(mats, gsc[i], preferred_element_type=F32)
        sides = lax.dot_general(mats, hsc[...], NT, preferred_element_type=F32)
        for n, a in enumerate(taps):
            h = a - 1 + i
            for b in range(3):
                at = slice((n * 3 + b) * chans, (n * 3 + b + 1) * chans)
                term = prod[at]
                if b == 0:
                    term = jnp.where(lane == cols - 1, sides[at, rows + i : rows + i + 1], pltpu.roll(term, cols - 1, 1))
                elif b == 2:
                    term = jnp.where(lane == 0, sides[at, i : i + 1], pltpu.roll(term, 1, 1))
                sums[h] = term if sums[h] is None else sums[h] + term
    for h in range(rows):
        out[h] = sums[h].astype(BF16)


class Order:
    def __init__(self):
        self.last = None

    def __call__(self, value):
        if self.last is not None:
            value, _ = lax.optimization_barrier((value, self.last))
        self.last = jax.tree.leaves(value)[0]
        return value


def doubled(got, own, late):
    return [jnp.where(late, got, own), jnp.where(late, own, got)]


def in_order(values, late):
    for b, swap in enumerate(late):
        values = [jnp.where(swap, values[n ^ 1 << b], values[n]) for n in range(len(values))]
    return values


def scaled(values, power):
    return (values * jnp.exp2(TOP - power)).astype(F16)


def added(total, got):
    count = total.shape[0]
    return total + got[:count].astype(F32) * jnp.exp2(got[count : count + 1].astype(F32) - TOP)


def chunk_stages(send, keep, finish, order, late, direct, halves, arrived):
    others = 1 << len(late) - 1
    lanes = send.shape[1]
    total, power = keep[:-POWER], keep[-1:]
    piece = total.shape[0] // others

    message = send.astype(F16)
    got = exchange(order(message), "width", 1)
    yield None
    got = order(got)
    yield None
    arrived.append(got[-EDGE:])
    total = added(total, got)
    power = jnp.maximum(power, got[-POWER - EDGE : -POWER - EDGE + 1].astype(F32)) + 1.0
    ends = jnp.concatenate(doubled(got[-EDGE:], message[-EDGE:], late[0]), axis=0)
    tail = jnp.broadcast_to(power, (POWER, lanes)).astype(F16)
    messages = []
    for n in range(1, others):
        part = scaled(total[n * piece : (n + 1) * piece], power)
        messages.append(jnp.concatenate([part, tail, ends], axis=0))
    messages = order(messages)
    gots = [exchange(messages[n - 1], "width", 2 * n) for n in range(1, others)]
    yield None
    gots = order(gots)
    yield None
    total = total[:piece]
    for got in gots:
        total = added(total, got)
    every = in_order([ends] + [got[piece + POWER :] for got in gots], late[1:])
    every = jnp.concatenate([v.reshape(2, EDGE, lanes) for v in every], axis=0).astype(F32)
    own = order(finish(total, every).astype(F16))
    if not direct:
        own = own[None]
        bits = [*reversed(range(2, len(late))), 0, 1]
        tiles = [0]
        for b in bits:
            got = exchange(own, "width", 1 << b)
            yield None
            got = order(got)
            yield None
            own = order(jnp.concatenate([own, got], axis=0))
            tiles += [tile ^ 1 << b for tile in tiles]
        yield [(unpacked(own), tiles)]
        return
    own = [own] + [exchange(own, "width", 2 * n) for n in range(1, others)]
    yield None
    gots = []
    for part in (range(others // 2), range(others // 2, others)) if halves else (range(others),):
        tiles = [2 * n for n in part]
        part = order([own[n] for n in part])
        yield None
        part = order(jnp.stack(part))
        gots.append((part, exchange(part, "width", 1), tiles))
    parts = []
    for part, got, tiles in gots:
        yield None
        parts += [(unpacked(part), tiles), (unpacked(order(got)), [tile ^ 1 for tile in tiles])]
    yield parts


def unpacked(every):
    rows = every.shape[1] - POWER
    scale = jnp.exp2(every[:, rows : rows + 1].astype(F32) - TOP)
    return (every[:, :rows].astype(F32) * scale).reshape(-1, every.shape[2])


FIRST = (0.0, 1.9, 2.0, 3.9, 4.0, 4.6, 4.62, 5.5, 5.52, 7.9)
LATER = (1.95, 3.85, 4.05, 5.95, 6.05, 6.5, 6.6, 6.7, 9.9, 10.0)
FORWARD = (0.1, 0.2, 2.7, 4.06, 5.94, 6.45)
BACKWARD = (6.72, 9.6)
PARTNERS = 0.3
AFTER = 2.0
DIRECT = (False, True)
SPLIT = True
HALVES = (False, True)


def chunk_times(j, steps):
    base = FIRST if j == 0 else [now + AFTER * (j - 1) for now in LATER]
    return base


def body(activations, filters, cotangent):
    chans, rows, cols = activations.shape
    block = cotangent.shape[0]
    outs = filters.shape[3]
    groups, width = lax.axis_size("chan"), lax.axis_size("width")
    lanes = 2 * block
    late = [((lax.axis_index("width") >> b) & 1) == 1 for b in range(bits_of(width))]
    swaps = [((lax.axis_index("chan") >> b) & 1) == 1 for b in range(1, bits_of(groups))]
    cotangent, late, swaps = lax.optimization_barrier((cotangent, late, swaps))
    mats = jnp.transpose(filters, (1, 2, 0, 3))
    pairs_of_rows = sum(0 <= h + a - 1 < rows for h in range(rows) for a in range(3))
    flops = 2 * pairs_of_rows * 3 * chans * cols * outs
    piece = -(-9 * chans // width)
    piece = -(-piece // 16) * 16
    factor = 1.0 / math.sqrt(rows * cols * width)
    order = Order()
    ends, arrived = {}, []

    def shifted(*sides):
        shapes = [((rows, 3 * chans, cols), BF16), ((2, rows * chans), BF16)]
        return call(taps_kernel, "shifted_taps", shapes, [], 0, activations, *sides)

    def filter_chunk(j):
        send, keep = call(
            functools.partial(filter_kernel, factor, piece, j == 0),
            "filter_terms",
            [((width // 2 * piece + POWER + EDGE, lanes), F32), ((width // 2 * piece + POWER, lanes), F32)],
            [((rows, lanes, cols), BF16), ((width * piece, lanes), F32)],
            flops * 2 // groups,
            bare,
            g[2 * j],
            g[2 * j + 1],
        )

        def finish(total, arrived):
            ends[j] = arrived
            body = functools.partial(border_kernel, factor)
            shape = ((piece + POWER, lanes), F32)
            return call(body, "border_terms", [shape], [((width * piece, lanes), F32)], 0, total, ends[0], ends[j])

        return chunk_stages(send, keep, finish, order, late, DIRECT[min(j, 1)], HALVES[min(j, 1)], arrived)

    def forward():
        odd = late[0]
        pairs = [(i, i + 1) for i in range(1, width - 1, 2)]
        mine = jnp.where(odd, columns[1:2], columns[0:1])
        far = lax.ppermute(order(mine), "width", pairs + [(j, i) for i, j in pairs])
        yield None
        far = order(far)
        yield None
        near = order(arrived[0]).astype(F32)
        near = (jnp.where(odd, near[3:4], near[2:3]) * jnp.exp2(near[0:1] - TOP)).astype(BF16)
        left, right = jnp.where(odd, near, far), jnp.where(odd, far, near)
        send, keep = call(
            forward_kernel,
            "forward_terms",
            [((groups // 2, rows, block, cols), F32)] * 2,
            [((outs, cols), F32)],
            flops,
            shifted(left, right)[0],
            mats.reshape(3, 3 * chans, outs),
        )
        for b in range(bits_of(groups) - 1):
            got = exchange(order(send), "chan", 1 << b)
            yield None
            total = keep + order(got)
            keep, send = total[: total.shape[0] // 2], total[total.shape[0] // 2 :]
        hop = 1 << bits_of(groups) - 1
        gots = [exchange(order(send[0, h]), "chan", hop) for h in range(rows)] if SPLIT else []
        sums = []
        for h in range(rows):
            got = gots[h] if SPLIT else exchange(order(send[0, h]), "chan", hop)
            yield None
            sums.append((keep[0, h] + order(got)).astype(BF16))
        result["conv"] = jnp.transpose(jnp.stack(sums), (1, 0, 2))

    def backward():
        out = call(
            input_kernel,
            "input_terms",
            [((rows, chans, cols), BF16)],
            [((rows, outs, cols), BF16), ((16, outs), BF16)],
            flops,
            mats.reshape(9 * chans, outs),
            jnp.stack([order(ends[j]) for j in range(groups // 2)]),
            *[g[r] for r in range(groups)],
        )
        yield None
        result["grad"] = order(jnp.transpose(out, (1, 0, 2)))

    def chunk(j):
        if j:
            g[2 * j + 1] = order(g[2 * j + 1])
        stages = filter_chunk(j)
        for piece in stages:
            pieces[j] = piece
            yield None

    def partners():
        for r in sorted(g):
            if r > 1:
                g[r | 1] = exchange(order(g[r]), "chan", 1)
        yield None

    g = {0: order(jnp.transpose(cotangent, (1, 0, 2)))}
    g[1] = exchange(g[0], "chan", 1)
    for b in reversed(range(1, bits_of(groups))):
        for r in [r for r in sorted(g) if r != 1]:
            g[r | 1 << b] = exchange(g[r], "chan", 1 << b)
    bare, columns = shifted()
    pieces, result = {}, {}
    hops = bits_of(groups)
    turns = []
    for j in range(groups // 2):
        stages = chunk(j)
        turns += [(now, stages) for now in chunk_times(j, bits_of(width))]
    conv = forward()
    extra = AFTER * (groups // 2 - 2)
    turns += [(FORWARD[0], conv), (FORWARD[1], conv), (PARTNERS, partners()), (FORWARD[2], conv)]
    turns += [(FORWARD[3] + b, conv) for b in range(hops - 1)]
    turns += [(FORWARD[4] + hops - 2, conv), (FORWARD[5] + hops - 2, conv), (FORWARD[5] + hops - 1.99, conv)]
    grad = backward()
    turns += [(BACKWARD[0] + extra, grad), (BACKWARD[1] + extra, grad)]
    for now, stages in sorted(turns, key=lambda turn: turn[0]):
        next(stages, None)
    for stages in dict.fromkeys(stages for _, stages in turns):
        for _ in stages:
            pass
    conv_output, input_grad = result["conv"], result["grad"]
    pieces = [pieces[j] for j in range(groups // 2)]

    if lanes % LANES:
        for j in range(len(pieces)):
            terms = {}
            for part, owners in pieces[j]:
                terms.update(zip(owners, jnp.split(part, len(owners), axis=0)))
            terms = in_order([terms[n] for n in range(width)], late)
            pieces[j] = jnp.concatenate([terms[p // (width // 2) + 2 * (p % (width // 2))] for p in range(width)], axis=0)
        for b in range(bits_of(groups // 2)):
            pieces = [jnp.where(swaps[b], pieces[j ^ 1 << b], pieces[j]) for j in range(len(pieces))]
        grads = jnp.concatenate(pieces, axis=1)
    else:
        parts = [part for chunk in pieces for part, _ in chunk]
        layout = [(j, owners) for j, chunk in enumerate(pieces) for _, owners in chunk]
        grads = pl.pallas_call(
            functools.partial(place_kernel, piece, layout),
            out_shape=jax.ShapeDtypeStruct((width * piece, outs), F32),
            in_specs=[VMEM] * len(parts),
            out_specs=pl.BlockSpec(memory_space=pl.ANY),
            scratch_shapes=[pltpu.SemaphoreType.DMA((width * groups // 2,))],
            compiler_params=pltpu.CompilerParams(vmem_limit_bytes=16 << 20),
            name="place_pieces",
        )(*parts)
    grads = grads[: 9 * chans]
    grads = jnp.transpose(grads.reshape(3, 3, chans, outs), (2, 0, 1, 3))
    return conv_output, input_grad, grads


def solution(mesh):
    cols = P("chan", None, "width")
    mats = P("chan", None, None, None)
    return jax.shard_map(body, mesh=mesh, in_specs=(cols, mats, cols), out_specs=(cols, cols, mats), check_vma=False)
```
